512 devices in a mesh: sec: 32 (over x, z), strip: 16 (over y, core).
Axes of the slice: x: 4, y: 8, z: 8, core: 2. Of those that a mesh axis runs over, the one named last changes fastest.
Arguments:
- raw_image: bfloat16 [32, 512, 512], P('sec', 'strip'), may hold values from -6 to 6
- w_first: bfloat16 [9, 32], replicated, may hold values from -2 to 2
- gain_one: float32 [32], replicated, may hold values from 0.25 to 1.75
- w_second: bfloat16 [3, 32, 96], replicated, may hold values from -0.375 to 0.375
- gain_two: float32 [32], replicated, may hold values from 0.25 to 1.75
- offsets: int32 [32, 2], replicated, may hold values from -8 to 8, as said below
- w_third: bfloat16 [9, 32, 96], replicated, may hold values from -0.21875 to 0.21875
- w_fourth: bfloat16 [9, 32, 96], replicated, may hold values from -0.21875 to 0.21875
Outputs:
- volume_out: float32 [32, 32, 256, 256], P('sec', None, 'strip')
The draws below stay inside these ranges and needn't reach their ends.
Inputs may be any that keep to these rules, and one draw needn't show every extreme that they name: `offsets`: every entry lies in -8 to 8; in both columns some section has exactly 8 and another exactly -8.
All inputs are finite; a program needn't handle non-finite values.
Results may differ from the reference program's by a relative error of at most 0.0051.
Values may be sent and summed in bfloat16 or wider, within the bound.
A program may use at most 64 MiB of HBM per device.

```python
import jax
import jax.numpy as jnp
from jax import lax

C = 32
COLUMNS = 512
OFF = 8
SECTIONS = 32
RAW_ROWS = 512
HEIGHT = 256
BREADTH = 256
BLOCKS = 32
BLOCK_W = 8


def draw_offsets(key, part):
    key = jax.random.fold_in(key, 11)
    key_vals, key_order = jax.random.split(key)
    values = jax.random.randint(key_vals, (SECTIONS, 2), -OFF, OFF + 1)
    order = jax.random.permutation(key_order, SECTIONS)
    places = jnp.arange(SECTIONS)
    upper = (places == order[0])[:, None]
    lower = (places == order[1])[:, None]
    values = jnp.where(upper, OFF, jnp.where(lower, -OFF, values))
    return values.astype(jnp.int32)


def levels(key, extent, cuts, low, largest):
    loudness, own = 1.0, jax.random.fold_in(key, 6)
    for dim, shards_of in cuts:
        steps = jnp.exp(jax.random.uniform(jax.random.fold_in(own, dim), (shards_of,), jnp.float32, low / len(cuts), largest / len(cuts)))
        loudness = loudness * jnp.repeat(steps, extent[dim] // shards_of).reshape([-1 if axis == dim else 1 for axis in range(len(extent))])
    return loudness


def gaussian(key, shape, width, reach, cuts=(), dtype=jnp.bfloat16):
    values = width * jax.random.normal(key, shape, jnp.float32)
    if cuts:
        values = values * levels(key, shape, cuts, -0.22, 0.18)
    return jnp.clip(values, -reach, reach).astype(dtype)


def setup_inputs(seed: int = 0) -> dict:
    seeds = jax.random.split(jax.random.key(seed), 9)
    return {
        "raw_image": gaussian(seeds[0], (SECTIONS, RAW_ROWS, COLUMNS), 1.0, 6.0, ((0, 32), (1, 16))),
        "w_first": gaussian(seeds[1], (9, C), 9 ** -0.5, 2.0),
        "gain_one": jnp.clip(1.0 + 0.15 * jax.random.normal(seeds[2], (C,), jnp.float32), 0.25, 1.75),
        "w_second": gaussian(seeds[3], (3, C, 3 * C), (9 * C) ** -0.5, 0.375),
        "gain_two": jnp.clip(1.0 + 0.15 * jax.random.normal(seeds[4], (C,), jnp.float32), 0.25, 1.75),
        "offsets": draw_offsets(jax.random.fold_in(seeds[8], 71), 0),
        "w_third": gaussian(seeds[6], (9, C, 3 * C), (27 * C) ** -0.5, 0.21875),
        "w_fourth": gaussian(seeds[7], (9, C, 3 * C), (27 * C) ** -0.5, 0.21875),
    }


def normalize(h, gain):
    v = jax.nn.silu(h)
    ms = lax.optimization_barrier(jnp.mean(v * v, axis=1, keepdims=True))
    return v / jnp.sqrt(1.0 + ms) * gain[None, :, None, None]

def reference(raw_image, w_first, gain_one, w_second, gain_two, offsets, w_third, w_fourth):
    high = lax.Precision.HIGHEST
    image = raw_image.astype(jnp.float32)[:, None]
    kernel_one = w_first.astype(jnp.float32).T.reshape(C, 1, 3, 3)
    first = lax.conv_general_dilated(image, kernel_one, (2, 2), ((1, 1), (1, 1)), dimension_numbers=('NCHW', 'OIHW', 'NCHW'), precision=high)
    level_one = normalize(first, gain_one).astype(jnp.bfloat16)
    kernel_two = w_second.astype(jnp.float32).reshape(3, C, 3, C).transpose(1, 3, 0, 2)
    second = lax.conv_general_dilated(level_one.astype(jnp.float32), kernel_two, (1, 1), ((1, 1), (1, 1)), dimension_numbers=('NCHW', 'OIHW', 'NCHW'), precision=high)
    feature = normalize(second, gain_two).astype(jnp.bfloat16)
    padded = jnp.pad(feature, ((0, 0), (0, 0), (OFF, OFF), (OFF, OFF)))

    def place(plane, shift):
        return lax.dynamic_slice(plane, (shift[0] * 0, OFF + shift[0], OFF + shift[1]), (C, HEIGHT, BREADTH))
    aligned = jax.vmap(place)(padded, offsets)

    def conv_three(volume, weight):
        kernel = weight.astype(jnp.float32).reshape(3, 3, C, 3, C).transpose(2, 4, 3, 0, 1)
        data = volume.astype(jnp.float32).transpose(1, 0, 2, 3)[None]
        result = lax.conv_general_dilated(data, kernel, (1, 1, 1), ((1, 1), (1, 1), (1, 1)), dimension_numbers=('NCDHW', 'OIDHW', 'NCDHW'), precision=high)
        return result[0].transpose(1, 0, 2, 3)
    middle = jax.nn.silu(conv_three(aligned, w_third)).astype(jnp.bfloat16)
    volume = conv_three(middle, w_fourth)
    grouped = volume.reshape(SECTIONS, C, HEIGHT, BLOCKS, BLOCK_W).transpose(3, 0, 2, 1, 4)
    return grouped.reshape(BLOCKS, SECTIONS, HEIGHT, C * BLOCK_W)
```

```python
import jax
import jax.numpy as jnp
from jax import lax
from jax.experimental import pallas as pl
from jax.experimental.pallas import tpu as pltpu
from jax.sharding import PartitionSpec as P

C = 32
SECS = 32
BLOCK = 8
ROWS = 16
EXTENT = 256
RAW = 512
STRIPS = 16

F32, BF16 = jnp.float32, jnp.bfloat16
MESH_ID = pl.DeviceIdType.MESH


def iota(shape, axis):
    return lax.broadcasted_iota(jnp.int32, shape, axis)


def dot_nn(a, b):
    return jnp.dot(a, b, preferred_element_type=F32)


def dot_nt(a, b):
    return lax.dot_general(a, b, (((1,), (1,)), ((), ())), preferred_element_type=F32)


def silu(u):
    half = 0.5 * u
    return half + half * jnp.tanh(half)


def widen(ref, small, rows, count):
    ref[0:rows, :] = jnp.zeros((rows, 128), F32)
    ref[0:rows, 0:count] = small.astype(F32)
    return ref[0:rows, :]


def build_first(w_first, tile, band_one):
    base = widen(tile, w_first[...], 9, C)
    base = base + pltpu.roll(base, 32, 1)
    base = base + pltpu.roll(base, 64, 1)
    taps = jnp.concatenate([base] * 4, axis=1)
    lane = iota((32, 512), 1)
    column = 6 * (lane // 256) + (lane % 256) // 32
    shift = iota((32, 512), 0) - 1 - 2 * column
    band_one[...] = jnp.zeros(band_one.shape, BF16)
    for a, start in ((0, 32), (1, 128), (2, 160)):
        block = jnp.zeros((32, 512), F32)
        for b in range(3):
            block = jnp.where(shift == b, taps[3 * a + b : 3 * a + b + 1, :], block)
        for half in range(2):
            band_one[half, start + 64 * half : start + 64 * half + 32, :] = block.astype(BF16)


def build_gain(gain, tile):
    base = widen(tile, gain[...], 1, C)
    base = base + pltpu.roll(base, 32, 1)
    return base + pltpu.roll(base, 64, 1)


def build_second(w_second, wide, band_two):
    wide[...] = jnp.zeros(wide.shape, F32)
    for a in range(3):
        wide[:, 0:96] = w_second[a].astype(F32)
        base = wide[:, 0:256]
        for x in range(6):
            block = pltpu.roll(base, 32 * x, 1).astype(BF16) if x else base.astype(BF16)
            band_two[0, 32 * x : 32 * x + 32, 256 * a : 256 * a + 256] = block
            band_two[1, 64 + 32 * x : 96 + 32 * x, 256 * a : 256 * a + 256] = block
        band_two[0, 192:256, 256 * a : 256 * a + 256] = jnp.zeros((64, 256), BF16)
        band_two[1, 0:64, 256 * a : 256 * a + 256] = jnp.zeros((64, 256), BF16)


def tap_base(weight, wide, a, b):
    lane = iota((C, 128), 1)
    total = jnp.zeros((C, 128), F32)
    for e in range(3):
        wide[:, 0:96] = weight[3 * b + e].astype(F32)
        part = wide[:, 0:128]
        turn = (32 * (e - a)) % 128
        part = pltpu.roll(part, turn, 1) if turn else part
        total = jnp.where(lane // 32 == e, part, total)
    return jnp.concatenate([total, jnp.zeros((C, 256), F32)], axis=1)


def build_third(w_third, wide, band_three):
    wide[...] = jnp.zeros(wide.shape, F32)
    for a in range(3):
        for b in range(3):
            base = tap_base(w_third, wide, a, b)[:, 0:256]
            where = 3 * b + a
            for x in range(6):
                block = pltpu.roll(base, 32 * x, 1).astype(BF16) if x else base.astype(BF16)
                band_three[where, 32 * x : 32 * x + 32, :] = block
                if x >= 4:
                    band_three[where, 64 + 32 * x : 96 + 32 * x, :] = block


def build_fourth(w_fourth, wide, band_four):
    wide[...] = jnp.zeros(wide.shape, F32)
    row = iota((256, 256), 0)
    order = jnp.where(iota((256, 256), 1) == (row % BLOCK) * C + row // BLOCK, 1.0, 0.0).astype(BF16)
    for b in range(3):
        edges = []
        for a in range(3):
            base = tap_base(w_fourth, wide, a, b)
            stack = [
                (pltpu.roll(base, 32 * x, 1) if x else base).astype(BF16) for x in range(BLOCK)
            ]
            band = dot_nn(order, jnp.concatenate(stack, axis=0))
            band_four[b, :, 256 * a : 256 * a + 256] = band[:, 0:256].astype(BF16)
            edges.append(band[:, 256:384])
        band_four[b, :, 768:896] = (edges[0] + pltpu.roll(edges[1], 64, 1)).astype(BF16)
        band_four[b, :, 896:1024] = edges[2].astype(BF16)


def pick_rows(strip, dy):
    m = iota((64, 96), 0)
    half, parity, q = m // 32, (m // 16) % 2, m % 16
    row = 2 * (dy - 4 + 11 * half + q) + parity
    inside = (row + 32 * strip >= 0) & (row + 32 * strip < RAW)
    return jnp.where(inside & (iota((64, 96), 1) - 32 == row), 1.0, 0.0).astype(BF16)


def cut_windows(rows, dx, send):
    padded = jnp.concatenate([rows, jnp.zeros((64, 128), F32)], axis=1)
    shifted = pltpu.roll(padded, lax.rem(648 - 2 * dx, 640), 1)
    lane = iota((16, 128), 1)
    low = (lane // 64) == 0
    even = (lane // 32) % 2 == 0
    for odd in range(2):
        view = pltpu.roll(shifted, 624, 1) if odd else shifted
        for tile in range(4):
            parts = [view[16 * p : 16 * p + 16, 128 * tile : 128 * tile + 128] for p in range(4)]
            for m1 in range(2):
                pair = []
                for h0 in range(2):
                    first, second = parts[h0], parts[2 + h0]
                    if m1 == 0:
                        pair.append(jnp.where(low, first, pltpu.roll(second, 64, 1)))
                    else:
                        pair.append(jnp.where(low, pltpu.roll(first, 64, 1), second))
                group = 4 * tile + 2 * m1
                here = jnp.where(even, pair[0], pltpu.roll(pair[1], 32, 1))
                then = jnp.where(even, pltpu.roll(pair[0], 96, 1), pair[1])
                send[2 * group + odd] = here.astype(BF16)
                send[2 * (group + 1) + odd] = then.astype(BF16)


def first_layer(recv, band_one, gain, offsets, strip, block, stage, lhs, big, square, mean, level):
    stage[...] = recv[...].reshape(SECS * 16, 128).astype(F32)
    for q in range(12):
        piece = stage[pl.ds(q, SECS, stride=16), :].astype(BF16)
        if q < 11:
            lhs[32 * q : 32 * q + 32, 0:128] = piece
        if q > 0:
            lhs[32 * q - 32 : 32 * q, 128:256] = piece
    dy, dx = offsets[:, 0:1], offsets[:, 1:2]
    lane = iota((SECS, 512), 1)
    column = 6 * (lane // 256) + (lane % 256) // 32
    scale = jnp.where(column + dx + (BLOCK * block - 3) < EXTENT, jnp.concatenate([gain] * 4, axis=1), 0.0)
    for half in range(2):
        big[352 * half : 352 * half + 352, :] = dot_nn(lhs[...], band_one[half])
    normalize(big, square, mean, 22, 512)

    def finish(i, _):
        at = pl.ds(pl.multiple_of(32 * i, 32), 32)
        y = big[at, :] * lax.rsqrt(1.0 + mean[at, :]) * scale
        y = jnp.where(dy + (ROWS * strip - 3 + i) < EXTENT, y, 0.0)
        level[at, :] = y.astype(BF16)
        return 0

    lax.fori_loop(0, 22, finish, 0)


def normalize(big, square, mean, count, lanes):
    def one(i, _):
        at = pl.ds(pl.multiple_of(32 * i, 32), 32)
        v = silu(big[at, 0:lanes])
        big[at, 0:lanes] = v
        square[at, 0:lanes] = (v * v).astype(BF16)
        return 0

    lax.fori_loop(0, count, one, 0)
    same = iota((128, 128), 0) // C == iota((128, 128), 1) // C
    spread = jnp.where(same, 1.0 / C, 0.0).astype(BF16)
    for g in range(lanes // 128):
        mean[0 : 32 * count, 128 * g : 128 * g + 128] = dot_nn(
            square[0 : 32 * count, 128 * g : 128 * g + 128], spread
        )


def shift_sections(y, wide_lanes):
    s = iota((SECS, wide_lanes), 0)
    before = jnp.where(s == 0, 0.0, pltpu.roll(y, 1, 0))
    after = jnp.where(s == SECS - 1, 0.0, pltpu.roll(y, SECS - 1, 0))
    return before, after


def second_layer(level, band_two, gain, offsets, strip, block, big, square, mean, columns):
    parts = []
    for g in range(2):
        lhs = jnp.concatenate(
            [level[32 * a : 32 * a + 640, 256 * g : 256 * g + 256] for a in range(3)], axis=1
        )
        parts.append(dot_nt(lhs, band_two[g]))
    big[0:640, 0:128] = parts[0][:, 0:128]
    big[0:640, 128:256] = parts[0][:, 128:256] + parts[1][:, 0:128]
    big[0:640, 256:384] = parts[1][:, 128:256]
    normalize(big, square, mean, 20, 384)
    dy, dx = offsets[:, 0:1], offsets[:, 1:2]
    placed = iota((SECS, 384), 1) // C + (BLOCK * block - 2)
    inside = (placed >= 0) & (placed < EXTENT) & (placed + dx >= 0) & (placed + dx < EXTENT)
    scale = jnp.where(inside, jnp.concatenate([gain] * 3, axis=1), 0.0)

    def finish(i, _):
        at = pl.ds(pl.multiple_of(32 * i, 32), 32)
        y = big[at, 0:384] * lax.rsqrt(1.0 + mean[at, 0:384]) * scale
        row = ROWS * strip - 2 + i
        y = jnp.where((dy + row >= 0) & (dy + row < EXTENT), y, 0.0)
        y = jnp.where((row >= 0) & (row < EXTENT), y, 0.0)
        before, after = shift_sections(y, 384)
        columns[at, 0:384] = before.astype(BF16)
        columns[at, 384:768] = y.astype(BF16)
        columns[at, 768:1152] = after.astype(BF16)
        return 0

    lax.fori_loop(0, 20, finish, 0)


def third_layer(columns, band_three, strip, block, big, middle):
    for g in range(2):
        total = None
        for b in range(3):
            for a in range(3):
                lhs = columns[32 * b : 32 * b + 576, 384 * a + 128 * g : 384 * a + 128 * g + 256]
                rhs = band_three[3 * b + a]
                term = dot_nt(lhs, rhs if g else rhs[0:128])
                total = term if total is None else total + term
        if g:
            big[0:576, 128:384] = total
        else:
            big[0:576, 0:128] = total
    lane = iota((SECS, 384), 1)
    column = jnp.where(lane < 320, lane, lane - 64) // C + (BLOCK * block - 1)
    inside = (column >= 0) & (column < EXTENT)
    low = iota((SECS, 128), 1) < 64

    def finish(i, _):
        at = pl.ds(pl.multiple_of(32 * i, 32), 32)
        row = ROWS * strip - 1 + i
        y = silu(big[at, 0:384])
        y = jnp.where(inside & (row >= 0) & (row < EXTENT), y, 0.0)
        before, after = shift_sections(y, 384)
        middle[at, 0:256] = before[:, 0:256].astype(BF16)
        middle[at, 256:512] = y[:, 0:256].astype(BF16)
        middle[at, 512:768] = after[:, 0:256].astype(BF16)
        middle[at, 768:896] = jnp.where(low, before[:, 256:384], y[:, 256:384]).astype(BF16)
        middle[at, 896:1024] = after[:, 256:384].astype(BF16)
        return 0

    lax.fori_loop(0, 18, finish, 0)


def fourth_layer(middle, band_four, big, out):
    total = None
    for b in range(3):
        term = dot_nt(middle[32 * b : 32 * b + 512, :], band_four[b])
        total = term if total is None else total + term
    big[0:512, 0:256] = total
    for i in range(ROWS):
        out[:, i, :] = big[32 * i : 32 * i + 32, 0:256]


def kernel(
    raw, w_first, gain_one, w_second, gain_two, offsets, offsets_smem, w_third, w_fourth, out,
    ext, send, recv, band_one, band_two, band_three, band_four, tile, wide, stage, lhs, big, square,
    mean, level, columns, middle, halo_send, halo_recv, pass_send, pass_recv,
):
    me, strip = lax.axis_index("sec"), lax.axis_index("strip")
    up = lax.rem(strip + STRIPS - 1, STRIPS)
    down = lax.rem(strip + 1, STRIPS)

    barrier = pltpu.get_barrier_semaphore()
    for near in (up, down):
        pl.semaphore_signal(barrier, inc=1, device_id={"strip": near}, device_id_type=MESH_ID)
    for d in range(1, SECS):
        peer = lax.rem(me + d, SECS)
        pl.semaphore_signal(barrier, inc=1, device_id={"sec": peer}, device_id_type=MESH_ID)

    ext[32:64, :] = raw[...]
    pl.semaphore_wait(barrier, SECS + 1)

    halos = []
    for n, (near, start) in enumerate(((down, 0), (up, 64))):
        copy = pltpu.make_async_remote_copy(
            src_ref=ext.at[32:64, :], dst_ref=ext.at[start : start + 32, :],
            send_sem=halo_send.at[n], recv_sem=halo_recv.at[n],
            device_id={"strip": near}, device_id_type=MESH_ID,
        )
        copy.start()
        halos.append(copy)
    build_first(w_first, tile, band_one)
    build_second(w_second, wide, band_two)
    dy, dx = offsets_smem[me, 0], offsets_smem[me, 1]
    chosen = pick_rows(strip, dy)
    for copy in halos:
        copy.wait()
    cut_windows(dot_nn(chosen, ext[...]), dx, send)

    for d in range(1, SECS):
        peer = lax.rem(me + d, SECS)
        pltpu.make_async_remote_copy(
            src_ref=send.at[peer], dst_ref=recv.at[me], send_sem=pass_send, recv_sem=pass_recv,
            device_id={"sec": peer}, device_id_type=MESH_ID,
        ).start()
    recv[me] = send[me]
    build_third(w_third, wide, band_three)
    build_fourth(w_fourth, wide, band_four)
    gain_a, gain_b = build_gain(gain_one, tile), build_gain(gain_two, tile)
    pltpu.make_async_copy(send.at[0 : SECS - 1], recv.at[0 : SECS - 1], pass_recv).wait()
    pltpu.make_async_copy(send.at[0 : SECS - 1], recv.at[0 : SECS - 1], pass_send).wait()

    first_layer(recv, band_one, gain_a, offsets, strip, me, stage, lhs, big, square, mean, level)
    second_layer(level, band_two, gain_b, offsets, strip, me, big, square, mean, columns)
    third_layer(columns, band_three, strip, me, big, middle)
    fourth_layer(middle, band_four, big, out)


def shards(raw_image, w_first, gain_one, w_second, gain_two, offsets, w_third, w_fourth):
    vmem = pl.BlockSpec(memory_space=pltpu.VMEM)
    smem = pl.BlockSpec(memory_space=pltpu.SMEM)
    result = pl.pallas_call(
        kernel,
        out_shape=jax.ShapeDtypeStruct((SECS, ROWS, C * BLOCK), F32),
        in_specs=[vmem] * 6 + [smem] + [vmem] * 2,
        out_specs=vmem,
        scratch_shapes=[
            pltpu.VMEM((96, RAW), BF16),
            pltpu.VMEM((SECS, 16, 128), BF16),
            pltpu.VMEM((SECS, 16, 128), BF16),
            pltpu.VMEM((2, 256, 512), BF16),
            pltpu.VMEM((2, 256, 768), BF16),
            pltpu.VMEM((9, 256, 256), BF16),
            pltpu.VMEM((3, 256, 1024), BF16),
            pltpu.VMEM((16, 128), F32),
            pltpu.VMEM((C, 256), F32),
            pltpu.VMEM((SECS * 16, 128), F32),
            pltpu.VMEM((352, 256), BF16),
            pltpu.VMEM((704, 512), F32),
            pltpu.VMEM((704, 512), BF16),
            pltpu.VMEM((704, 512), F32),
            pltpu.VMEM((704, 512), BF16),
            pltpu.VMEM((640, 1152), BF16),
            pltpu.VMEM((576, 1024), BF16),
            pltpu.SemaphoreType.DMA((2,)),
            pltpu.SemaphoreType.DMA((2,)),
            pltpu.SemaphoreType.DMA,
            pltpu.SemaphoreType.DMA,
        ],
        compiler_params=pltpu.CompilerParams(
            collective_id=0, has_side_effects=True, vmem_limit_bytes=48 * 2**20
        ),
        cost_estimate=pl.CostEstimate(flops=10**9, bytes_accessed=2**20, transcendentals=10**6),
    )(
        raw_image.reshape(32, RAW), w_first, gain_one.reshape(1, C), w_second,
        gain_two.reshape(1, C), offsets, offsets, w_third, w_fourth,
    )
    return result.reshape(1, SECS, ROWS, C * BLOCK)


def solution(mesh):
    placed = (P("sec", "strip", None), P(), P(), P(), P(), P(), P(), P())
    return jax.shard_map(
        shards, mesh=mesh, in_specs=placed, out_specs=P("sec", None, "strip", None), check_vma=False
    )
```

```python
import jax
import jax.numpy as jnp
from jax import lax
from jax.experimental import pallas as pl
from jax.experimental.pallas import tpu as pltpu
from jax.sharding import PartitionSpec as P

C = 32
SECS = 32
BLOCK = 8
ROWS = 16
EXTENT = 256
RAW = 512
STRIPS = 16

F32, BF16 = jnp.float32, jnp.bfloat16
MESH_ID = pl.DeviceIdType.MESH


PEERS = sorted(
    [(x, z) for x in range(4) for z in range(8) if x or z],
    key=lambda at: -(min(at[0], 4 - at[0]) + min(at[1], 8 - at[1])),
)


def peer_at(me, x, z):
    return lax.rem(me // 8 + x, 4) * 8 + lax.rem(lax.rem(me, 8) + z, 8)


def iota(shape, axis):
    return lax.broadcasted_iota(jnp.int32, shape, axis)


def dot_nn(a, b):
    return jnp.dot(a, b, preferred_element_type=F32)


def dot_nt(a, b):
    return lax.dot_general(a, b, (((1,), (1,)), ((), ())), preferred_element_type=F32)


def silu(u):
    half = 0.5 * u
    return half + half * jnp.tanh(half)


def widen(ref, small, rows, count):
    ref[0:rows, :] = jnp.zeros((rows, 128), F32)
    ref[0:rows, 0:count] = small.astype(F32)
    return ref[0:rows, :]


def build_first(w_first, tile, band_one):
    base = widen(tile, w_first[...], 9, C)
    base = base + pltpu.roll(base, 32, 1)
    base = base + pltpu.roll(base, 64, 1)
    taps = jnp.concatenate([base] * 4, axis=1)
    lane = iota((32, 512), 1)
    column = 6 * (lane // 256) + (lane % 256) // 32
    shift = iota((32, 512), 0) - 1 - 2 * column
    band_one[...] = jnp.zeros(band_one.shape, BF16)
    for a, start in ((0, 32), (1, 128), (2, 160)):
        block = jnp.zeros((32, 512), F32)
        for b in range(3):
            block = jnp.where(shift == b, taps[3 * a + b : 3 * a + b + 1, :], block)
        for half in range(2):
            band_one[half, start + 64 * half : start + 64 * half + 32, :] = block.astype(BF16)


def build_gain(gain, tile):
    base = widen(tile, gain[...], 1, C)
    base = base + pltpu.roll(base, 32, 1)
    return base + pltpu.roll(base, 64, 1)


def build_second(w_second, wide, band_two):
    wide[...] = jnp.zeros(wide.shape, F32)
    for a in range(3):
        wide[:, 0:96] = w_second[a].astype(F32)
        base = wide[:, 0:256]
        for x in range(6):
            block = pltpu.roll(base, 32 * x, 1).astype(BF16) if x else base.astype(BF16)
            band_two[0, 32 * x : 32 * x + 32, 256 * a : 256 * a + 256] = block
            band_two[1, 64 + 32 * x : 96 + 32 * x, 256 * a : 256 * a + 256] = block
        band_two[0, 192:256, 256 * a : 256 * a + 256] = jnp.zeros((64, 256), BF16)
        band_two[1, 0:64, 256 * a : 256 * a + 256] = jnp.zeros((64, 256), BF16)


def tap_base(weight, wide, a, b):
    lane = iota((C, 128), 1)
    total = jnp.zeros((C, 128), F32)
    for e in range(3):
        wide[:, 0:96] = weight[3 * b + e].astype(F32)
        part = wide[:, 0:128]
        turn = (32 * (e - a)) % 128
        part = pltpu.roll(part, turn, 1) if turn else part
        total = jnp.where(lane // 32 == e, part, total)
    return jnp.concatenate([total, jnp.zeros((C, 256), F32)], axis=1)


def build_third(w_third, wide, band_three):
    wide[...] = jnp.zeros(wide.shape, F32)
    for a in range(3):
        for b in range(3):
            base = tap_base(w_third, wide, a, b)[:, 0:256]
            where = 3 * b + a
            for x in range(6):
                block = pltpu.roll(base, 32 * x, 1).astype(BF16) if x else base.astype(BF16)
                band_three[where, 32 * x : 32 * x + 32, :] = block
                if x >= 4:
                    band_three[where, 64 + 32 * x : 96 + 32 * x, :] = block


def build_fourth(w_fourth, wide, band_four):
    wide[...] = jnp.zeros(wide.shape, F32)
    row = iota((256, 256), 0)
    order = jnp.where(iota((256, 256), 1) == (row % BLOCK) * C + row // BLOCK, 1.0, 0.0).astype(BF16)
    for b in range(3):
        edges = []
        for a in range(3):
            base = tap_base(w_fourth, wide, a, b)
            stack = [
                (pltpu.roll(base, 32 * x, 1) if x else base).astype(BF16) for x in range(BLOCK)
            ]
            band = dot_nn(order, jnp.concatenate(stack, axis=0))
            band_four[b, :, 256 * a : 256 * a + 256] = band[:, 0:256].astype(BF16)
            edges.append(band[:, 256:384])
        band_four[b, :, 768:896] = (edges[0] + pltpu.roll(edges[1], 64, 1)).astype(BF16)
        band_four[b, :, 896:1024] = edges[2].astype(BF16)


def pick_rows(strip, dy):
    m = iota((64, 96), 0)
    half, parity, q = m // 32, (m // 16) % 2, m % 16
    row = 2 * (dy - 4 + 11 * half + q) + parity
    inside = (row + 32 * strip >= 0) & (row + 32 * strip < RAW)
    return jnp.where(inside & (iota((64, 96), 1) - 32 == row), 1.0, 0.0).astype(BF16)


def cut_windows(rows, dx, send):
    padded = jnp.concatenate([rows, jnp.zeros((64, 128), F32)], axis=1)
    shifted = pltpu.roll(padded, lax.rem(648 - 2 * dx, 640), 1)
    lane = iota((16, 128), 1)
    low = (lane // 64) == 0
    even = (lane // 32) % 2 == 0
    for odd in range(2):
        view = pltpu.roll(shifted, 624, 1) if odd else shifted
        for tile in range(4):
            parts = [view[16 * p : 16 * p + 16, 128 * tile : 128 * tile + 128] for p in range(4)]
            for m1 in range(2):
                pair = []
                for h0 in range(2):
                    first, second = parts[h0], parts[2 + h0]
                    if m1 == 0:
                        pair.append(jnp.where(low, first, pltpu.roll(second, 64, 1)))
                    else:
                        pair.append(jnp.where(low, pltpu.roll(first, 64, 1), second))
                group = 4 * tile + 2 * m1
                here = jnp.where(even, pair[0], pltpu.roll(pair[1], 32, 1))
                then = jnp.where(even, pltpu.roll(pair[0], 96, 1), pair[1])
                send[2 * group + odd] = here.astype(BF16)
                send[2 * (group + 1) + odd] = then.astype(BF16)


def as_column(row):
    same = iota((SECS, SECS), 0) == iota((SECS, SECS), 1)
    return jnp.sum(jnp.where(same, row.astype(F32), 0.0), axis=1, keepdims=True).astype(jnp.int32)


def first_layer(recv, band_one, gain, offsets, strip, block, stage, lhs, big, square, mean, level):
    stage[...] = recv[...].reshape(SECS * 16, 128).astype(F32)
    for q in range(12):
        piece = stage[pl.ds(q, SECS, stride=16), :].astype(BF16)
        if q < 11:
            lhs[32 * q : 32 * q + 32, 0:128] = piece
        if q > 0:
            lhs[32 * q - 32 : 32 * q, 128:256] = piece
    dy, dx = as_column(offsets[0:1, :]), as_column(offsets[1:2, :])
    lane = iota((SECS, 512), 1)
    column = 6 * (lane // 256) + (lane % 256) // 32
    scale = jnp.where(column + dx + (BLOCK * block - 3) < EXTENT, jnp.concatenate([gain] * 4, axis=1), 0.0)
    for half in range(2):
        big[352 * half : 352 * half + 352, :] = dot_nn(lhs[...], band_one[half])
    normalize(big, square, mean, 22, 512)

    def finish(i, _):
        at = pl.ds(pl.multiple_of(32 * i, 32), 32)
        y = big[at, :] * lax.rsqrt(1.0 + mean[at, :]) * scale
        y = jnp.where(dy + (ROWS * strip - 3 + i) < EXTENT, y, 0.0)
        level[at, :] = y.astype(BF16)
        return 0

    lax.fori_loop(0, 22, finish, 0, unroll=True)


def normalize(big, square, mean, count, lanes):
    def one(i, _):
        at = pl.ds(pl.multiple_of(32 * i, 32), 32)
        v = silu(big[at, 0:lanes])
        big[at, 0:lanes] = v
        square[at, 0:lanes] = (v * v).astype(BF16)
        return 0

    lax.fori_loop(0, count, one, 0, unroll=True)
    same = iota((128, 128), 0) // C == iota((128, 128), 1) // C
    spread = jnp.where(same, 1.0 / C, 0.0).astype(BF16)
    for g in range(lanes // 128):
        mean[0 : 32 * count, 128 * g : 128 * g + 128] = dot_nn(
            square[0 : 32 * count, 128 * g : 128 * g + 128], spread
        )


def shift_sections(y, wide_lanes):
    s = iota((SECS, wide_lanes), 0)
    before = jnp.where(s == 0, 0.0, pltpu.roll(y, 1, 0))
    after = jnp.where(s == SECS - 1, 0.0, pltpu.roll(y, SECS - 1, 0))
    return before, after


def second_layer(level, band_two, gain, offsets, strip, block, big, square, mean, columns):
    parts = []
    for g in range(2):
        lhs = jnp.concatenate(
            [level[32 * a : 32 * a + 640, 256 * g : 256 * g + 256] for a in range(3)], axis=1
        )
        parts.append(dot_nt(lhs, band_two[g]))
    big[0:640, 0:128] = parts[0][:, 0:128]
    big[0:640, 128:256] = parts[0][:, 128:256] + parts[1][:, 0:128]
    big[0:640, 256:384] = parts[1][:, 128:256]
    normalize(big, square, mean, 20, 384)
    dy, dx = as_column(offsets[0:1, :]), as_column(offsets[1:2, :])
    placed = iota((SECS, 384), 1) // C + (BLOCK * block - 2)
    inside = (placed >= 0) & (placed < EXTENT) & (placed + dx >= 0) & (placed + dx < EXTENT)
    scale = jnp.where(inside, jnp.concatenate([gain] * 3, axis=1), 0.0)

    def finish(i, _):
        at = pl.ds(pl.multiple_of(32 * i, 32), 32)
        y = big[at, 0:384] * lax.rsqrt(1.0 + mean[at, 0:384]) * scale
        row = ROWS * strip - 2 + i
        y = jnp.where((dy + row >= 0) & (dy + row < EXTENT), y, 0.0)
        y = jnp.where((row >= 0) & (row < EXTENT), y, 0.0)
        before, after = shift_sections(y, 384)
        columns[at, 0:384] = before.astype(BF16)
        columns[at, 384:768] = y.astype(BF16)
        columns[at, 768:1152] = after.astype(BF16)
        return 0

    lax.fori_loop(0, 20, finish, 0, unroll=True)


def third_layer(columns, band_three, strip, block, big, middle):
    for g in range(2):
        total = None
        for b in range(3):
            for a in range(3):
                lhs = columns[32 * b : 32 * b + 576, 384 * a + 128 * g : 384 * a + 128 * g + 256]
                rhs = band_three[3 * b + a]
                term = dot_nt(lhs, rhs if g else rhs[0:128])
                total = term if total is None else total + term
        if g:
            big[0:576, 128:384] = total
        else:
            big[0:576, 0:128] = total
    lane = iota((SECS, 384), 1)
    column = jnp.where(lane < 320, lane, lane - 64) // C + (BLOCK * block - 1)
    inside = (column >= 0) & (column < EXTENT)
    low = iota((SECS, 128), 1) < 64

    def finish(i, _):
        at = pl.ds(pl.multiple_of(32 * i, 32), 32)
        row = ROWS * strip - 1 + i
        y = silu(big[at, 0:384])
        y = jnp.where(inside & (row >= 0) & (row < EXTENT), y, 0.0)
        before, after = shift_sections(y, 384)
        middle[at, 0:256] = before[:, 0:256].astype(BF16)
        middle[at, 256:512] = y[:, 0:256].astype(BF16)
        middle[at, 512:768] = after[:, 0:256].astype(BF16)
        middle[at, 768:896] = jnp.where(low, before[:, 256:384], y[:, 256:384]).astype(BF16)
        middle[at, 896:1024] = after[:, 256:384].astype(BF16)
        return 0

    lax.fori_loop(0, 18, finish, 0, unroll=True)


def fourth_layer(middle, band_four, big, out):
    total = None
    for b in range(3):
        term = dot_nt(middle[32 * b : 32 * b + 512, :], band_four[b])
        total = term if total is None else total + term
    big[0:512, 0:256] = total
    for i in range(ROWS):
        out[:, i, :] = big[32 * i : 32 * i + 32, 0:256]


def kernel(
    raw_hbm, w_first_hbm, gain_one_hbm, w_second_hbm, gain_two_hbm, offsets_hbm, w_third_hbm,
    w_fourth_hbm, out,
    w_first, gain_one, w_second, gain_two, offsets, w_third, w_fourth, offsets_smem,
    ext, send, recv, band_one, band_two, band_three, band_four, tile, wide, stage, lhs, big, square,
    mean, level, columns, middle, load_sem, halo_send, halo_recv, pass_send, pass_recv,
):
    me, strip = lax.axis_index("sec"), lax.axis_index("strip")
    up = lax.rem(strip + STRIPS - 1, STRIPS)
    down = lax.rem(strip + 1, STRIPS)

    loads = [
        pltpu.make_async_copy(source, target, load_sem.at[n])
        for n, (source, target) in enumerate(
            (
                (raw_hbm, ext.at[32:64, :]),
                (offsets_hbm, offsets_smem),
                (w_first_hbm, w_first),
                (w_second_hbm, w_second),
                (w_third_hbm, w_third),
                (w_fourth_hbm, w_fourth),
                (gain_one_hbm, gain_one),
                (gain_two_hbm, gain_two),
                (offsets_hbm, offsets),
            )
        )
    ]
    for load in loads:
        load.start()

    barrier = pltpu.get_barrier_semaphore()
    for near in (up, down):
        pl.semaphore_signal(barrier, inc=1, device_id={"strip": near}, device_id_type=MESH_ID)
    for x, z in PEERS:
        peer = peer_at(me, x, z)
        pl.semaphore_signal(barrier, inc=1, device_id={"sec": peer}, device_id_type=MESH_ID)

    for load in loads:
        load.wait()
    pl.semaphore_wait(barrier, SECS + 1)

    halos = []
    for n, (near, start) in enumerate(((down, 0), (up, 64))):
        copy = pltpu.make_async_remote_copy(
            src_ref=ext.at[32:64, :], dst_ref=ext.at[start : start + 32, :],
            send_sem=halo_send.at[n], recv_sem=halo_recv.at[n],
            device_id={"strip": near}, device_id_type=MESH_ID,
        )
        copy.start()
        halos.append(copy)
    build_first(w_first, tile, band_one)
    build_second(w_second, wide, band_two)
    dy, dx = offsets_smem[0, me], offsets_smem[1, me]
    chosen = pick_rows(strip, dy)
    for copy in halos:
        copy.wait_recv()
    cut_windows(dot_nn(chosen, ext[...]), dx, send)

    for x, z in PEERS:
        peer = peer_at(me, x, z)
        pltpu.make_async_remote_copy(
            src_ref=send.at[peer], dst_ref=recv.at[me], send_sem=pass_send, recv_sem=pass_recv,
            device_id={"sec": peer}, device_id_type=MESH_ID,
        ).start()
    recv[me] = send[me]
    build_third(w_third, wide, band_three)
    build_fourth(w_fourth, wide, band_four)
    gain_a, gain_b = build_gain(gain_one, tile), build_gain(gain_two, tile)
    pltpu.make_async_copy(send.at[0 : SECS - 1], recv.at[0 : SECS - 1], pass_recv).wait()
    pltpu.make_async_copy(send.at[0 : SECS - 1], recv.at[0 : SECS - 1], pass_send).wait()
    for copy in halos:
        copy.wait_send()

    first_layer(recv, band_one, gain_a, offsets, strip, me, stage, lhs, big, square, mean, level)
    second_layer(level, band_two, gain_b, offsets, strip, me, big, square, mean, columns)
    third_layer(columns, band_three, strip, me, big, middle)
    fourth_layer(middle, band_four, big, out)


def shards(raw_image, w_first, gain_one, w_second, gain_two, offsets, w_third, w_fourth):
    hbm = pl.BlockSpec(memory_space=pltpu.HBM)
    result = pl.pallas_call(
        kernel,
        out_shape=jax.ShapeDtypeStruct((SECS, ROWS, C * BLOCK), F32),
        in_specs=[hbm] * 8,
        out_specs=pl.BlockSpec(memory_space=pltpu.VMEM),
        scratch_shapes=[
            pltpu.VMEM((9, C), BF16),
            pltpu.VMEM((1, C), F32),
            pltpu.VMEM((3, C, 96), BF16),
            pltpu.VMEM((1, C), F32),
            pltpu.VMEM((2, SECS), jnp.int32),
            pltpu.VMEM((9, C, 96), BF16),
            pltpu.VMEM((9, C, 96), BF16),
            pltpu.SMEM((2, SECS), jnp.int32),
            pltpu.VMEM((96, RAW), BF16),
            pltpu.VMEM((SECS, 16, 128), BF16),
            pltpu.VMEM((SECS, 16, 128), BF16),
            pltpu.VMEM((2, 256, 512), BF16),
            pltpu.VMEM((2, 256, 768), BF16),
            pltpu.VMEM((9, 256, 256), BF16),
            pltpu.VMEM((3, 256, 1024), BF16),
            pltpu.VMEM((16, 128), F32),
            pltpu.VMEM((C, 256), F32),
            pltpu.VMEM((SECS * 16, 128), F32),
            pltpu.VMEM((352, 256), BF16),
            pltpu.VMEM((704, 512), F32),
            pltpu.VMEM((704, 512), BF16),
            pltpu.VMEM((704, 512), F32),
            pltpu.VMEM((704, 512), BF16),
            pltpu.VMEM((640, 1152), BF16),
            pltpu.VMEM((576, 1024), BF16),
            pltpu.SemaphoreType.DMA((9,)),
            pltpu.SemaphoreType.DMA((2,)),
            pltpu.SemaphoreType.DMA((2,)),
            pltpu.SemaphoreType.DMA,
            pltpu.SemaphoreType.DMA,
        ],
        compiler_params=pltpu.CompilerParams(
            collective_id=0, has_side_effects=True, vmem_limit_bytes=60 * 2**20
        ),
        cost_estimate=pl.CostEstimate(flops=10**9, bytes_accessed=2**20, transcendentals=10**6),
    )(
        raw_image.reshape(32, RAW), w_first, gain_one.reshape(1, C), w_second,
        gain_two.reshape(1, C), offsets.T, w_third, w_fourth,
    )
    return result.reshape(1, SECS, ROWS, C * BLOCK)


def solution(mesh):
    placed = (P("sec", "strip", None), P(), P(), P(), P(), P(), P(), P())
    return jax.shard_map(
        shards, mesh=mesh, in_specs=placed, out_specs=P("sec", None, "strip", None), check_vma=False
    )
```

```python
import jax
import jax.numpy as jnp
from jax import lax
from jax.experimental import pallas as pl
from jax.experimental.pallas import tpu as pltpu
from jax.sharding import PartitionSpec as P

C = 32
SECS = 32
BLOCK = 8
ROWS = 16
EXTENT = 256
RAW = 512
STRIPS = 16

F32, BF16 = jnp.float32, jnp.bfloat16
MESH_ID = pl.DeviceIdType.MESH


PEERS = sorted(
    [(x, z) for x in range(4) for z in range(8) if x or z],
    key=lambda at: -(min(at[0], 4 - at[0]) + min(at[1], 8 - at[1])),
)


def peer_at(me, x, z):
    return lax.rem(me // 8 + x, 4) * 8 + lax.rem(lax.rem(me, 8) + z, 8)


def iota(shape, axis):
    return lax.broadcasted_iota(jnp.int32, shape, axis)


def dot_nn(a, b):
    return jnp.dot(a, b, preferred_element_type=F32)


def dot_nt(a, b):
    return lax.dot_general(a, b, (((1,), (1,)), ((), ())), preferred_element_type=F32)


def silu(u):
    half = 0.5 * u
    return half + half * jnp.tanh(half)


def widen(ref, small, rows, count):
    ref[0:rows, :] = jnp.zeros((rows, 128), F32)
    ref[0:rows, 0:count] = small.astype(F32)
    return ref[0:rows, :]


def build_first(w_first, tile, band_one):
    base = widen(tile, w_first[...], 9, C)
    base = base + pltpu.roll(base, 32, 1)
    base = base + pltpu.roll(base, 64, 1)
    taps = jnp.concatenate([base] * 4, axis=1)
    lane = iota((32, 512), 1)
    column = 6 * (lane // 256) + (lane % 256) // 32
    shift = iota((32, 512), 0) - 1 - 2 * column
    band_one[...] = jnp.zeros(band_one.shape, BF16)
    for a, start in ((0, 32), (1, 128), (2, 160)):
        block = jnp.zeros((32, 512), F32)
        for b in range(3):
            block = jnp.where(shift == b, taps[3 * a + b : 3 * a + b + 1, :], block)
        for half in range(2):
            band_one[half, start + 64 * half : start + 64 * half + 32, :] = block.astype(BF16)


def build_gain(gain, tile):
    base = widen(tile, gain[...], 1, C)
    base = base + pltpu.roll(base, 32, 1)
    return base + pltpu.roll(base, 64, 1)


def build_second(w_second, wide, band_two):
    wide[...] = jnp.zeros(wide.shape, F32)
    for a in range(3):
        wide[:, 0:96] = w_second[a].astype(F32)
        base = wide[:, 0:256]
        for x in range(6):
            block = pltpu.roll(base, 32 * x, 1).astype(BF16) if x else base.astype(BF16)
            band_two[0, 32 * x : 32 * x + 32, 256 * a : 256 * a + 256] = block
            band_two[1, 64 + 32 * x : 96 + 32 * x, 256 * a : 256 * a + 256] = block
        band_two[0, 192:256, 256 * a : 256 * a + 256] = jnp.zeros((64, 256), BF16)
        band_two[1, 0:64, 256 * a : 256 * a + 256] = jnp.zeros((64, 256), BF16)


def tap_base(weight, wide, a, b):
    lane = iota((C, 128), 1)
    total = jnp.zeros((C, 128), F32)
    for e in range(3):
        wide[:, 0:96] = weight[3 * b + e].astype(F32)
        part = wide[:, 0:128]
        turn = (32 * (e - a)) % 128
        part = pltpu.roll(part, turn, 1) if turn else part
        total = jnp.where(lane // 32 == e, part, total)
    return jnp.concatenate([total, jnp.zeros((C, 256), F32)], axis=1)


def build_third(w_third, wide, band_three):
    wide[...] = jnp.zeros(wide.shape, F32)
    for a in range(3):
        for b in range(3):
            base = tap_base(w_third, wide, a, b)[:, 0:256]
            where = 3 * b + a
            for x in range(6):
                block = pltpu.roll(base, 32 * x, 1).astype(BF16) if x else base.astype(BF16)
                band_three[where, 32 * x : 32 * x + 32, :] = block
                if x >= 4:
                    band_three[where, 64 + 32 * x : 96 + 32 * x, :] = block


def build_fourth(w_fourth, wide, band_four):
    wide[...] = jnp.zeros(wide.shape, F32)
    row = iota((256, 256), 0)
    order = jnp.where(iota((256, 256), 1) == (row % BLOCK) * C + row // BLOCK, 1.0, 0.0).astype(BF16)
    for b in range(3):
        edges = []
        for a in range(3):
            base = tap_base(w_fourth, wide, a, b)
            stack = [
                (pltpu.roll(base, 32 * x, 1) if x else base).astype(BF16) for x in range(BLOCK)
            ]
            band = dot_nn(order, jnp.concatenate(stack, axis=0))
            band_four[b, :, 256 * a : 256 * a + 256] = band[:, 0:256].astype(BF16)
            edges.append(band[:, 256:384])
        band_four[b, :, 768:896] = (edges[0] + pltpu.roll(edges[1], 64, 1)).astype(BF16)
        band_four[b, :, 896:1024] = edges[2].astype(BF16)


def pick_rows(strip, dy):
    m = iota((64, 96), 0)
    half, parity, q = m // 32, (m // 16) % 2, m % 16
    row = 2 * (dy - 4 + 11 * half + q) + parity
    inside = (row + 32 * strip >= 0) & (row + 32 * strip < RAW)
    return jnp.where(inside & (iota((64, 96), 1) - 32 == row), 1.0, 0.0).astype(BF16)


def cut_windows(rows, dx, send):
    padded = jnp.concatenate([rows, jnp.zeros((64, 128), F32)], axis=1)
    shifted = pltpu.roll(padded, lax.rem(648 - 2 * dx, 640), 1)
    lane = iota((16, 128), 1)
    low = (lane // 64) == 0
    even = (lane // 32) % 2 == 0
    for odd in range(2):
        view = pltpu.roll(shifted, 624, 1) if odd else shifted
        for tile in range(4):
            parts = [view[16 * p : 16 * p + 16, 128 * tile : 128 * tile + 128] for p in range(4)]
            for m1 in range(2):
                pair = []
                for h0 in range(2):
                    first, second = parts[h0], parts[2 + h0]
                    if m1 == 0:
                        pair.append(jnp.where(low, first, pltpu.roll(second, 64, 1)))
                    else:
                        pair.append(jnp.where(low, pltpu.roll(first, 64, 1), second))
                group = 4 * tile + 2 * m1
                here = jnp.where(even, pair[0], pltpu.roll(pair[1], 32, 1))
                then = jnp.where(even, pltpu.roll(pair[0], 96, 1), pair[1])
                send[2 * group + odd] = here.astype(BF16)
                send[2 * (group + 1) + odd] = then.astype(BF16)


def as_column(row):
    same = iota((SECS, SECS), 0) == iota((SECS, SECS), 1)
    return jnp.sum(jnp.where(same, row.astype(F32), 0.0), axis=1, keepdims=True).astype(jnp.int32)


FIRST, SECOND, THIRD, FOURTH = (0, 11, 22), (0, 9, 20), (0, 9, 18), (0, 16)


def span(start, stop):
    return slice(32 * start, 32 * stop)


def gather_first(recv, stage, lhs):
    stage[...] = recv[...].reshape(SECS * 16, 128).astype(F32)
    for q in range(12):
        piece = stage[pl.ds(q, SECS, stride=16), :].astype(BF16)
        if q < 11:
            lhs[32 * q : 32 * q + 32, 0:128] = piece
        if q > 0:
            lhs[32 * q - 32 : 32 * q, 128:256] = piece


def normalize(big, square, start, stop, lanes):
    for i in range(start, stop):
        v = silu(big[span(i, i + 1), 0:lanes])
        big[span(i, i + 1), 0:lanes] = v
        square[span(i, i + 1), 0:lanes] = (v * v).astype(BF16)
    same = iota((256, 256), 0) // C == iota((256, 256), 1) // C
    spread = jnp.where(same, 1.0 / C, 0.0).astype(BF16)
    parts = []
    for low in range(0, lanes, 256):
        wide = min(256, lanes - low)
        parts.append(dot_nn(square[span(start, stop), low : low + wide], spread[0:wide, 0:wide]))
    return jnp.concatenate(parts, axis=1)


def shift_sections(y, wide_lanes):
    s = iota((SECS, wide_lanes), 0)
    before = jnp.where(s == 0, 0.0, pltpu.roll(y, 1, 0))
    after = jnp.where(s == SECS - 1, 0.0, pltpu.roll(y, SECS - 1, 0))
    return before, after


def first_multiply(half, lhs, band_one, big):
    big[span(11 * half, 11 * half + 11), :] = dot_nn(lhs[...], band_one[half])


def first_scale(gain, dx, block):
    lane = iota((SECS, 512), 1)
    column = 6 * (lane // 256) + (lane % 256) // 32
    inside = column + dx + (BLOCK * block - 3) < EXTENT
    return jnp.where(inside, jnp.concatenate([gain] * 4, axis=1), 0.0)


def first_finish(start, stop, scale, dy, strip, big, square, level):
    mean = normalize(big, square, start, stop, 512)
    for i in range(start, stop):
        y = big[span(i, i + 1), :] * lax.rsqrt(1.0 + mean[span(i - start, i - start + 1)]) * scale
        y = jnp.where(dy + (ROWS * strip - 3 + i) < EXTENT, y, 0.0)
        level[span(i, i + 1), :] = y.astype(BF16)


def second_multiply(start, stop, level, band_two, big):
    parts = []
    for g in range(2):
        lhs = jnp.concatenate(
            [level[span(start + a, stop + a), 256 * g : 256 * g + 256] for a in range(3)], axis=1
        )
        parts.append(dot_nt(lhs, band_two[g]))
    big[span(start, stop), 0:128] = parts[0][:, 0:128]
    big[span(start, stop), 128:256] = parts[0][:, 128:256] + parts[1][:, 0:128]
    big[span(start, stop), 256:384] = parts[1][:, 128:256]


def second_scale(gain, dx, block):
    placed = iota((SECS, 384), 1) // C + (BLOCK * block - 2)
    inside = (placed >= 0) & (placed < EXTENT) & (placed + dx >= 0) & (placed + dx < EXTENT)
    return jnp.where(inside, jnp.concatenate([gain] * 3, axis=1), 0.0)


def second_finish(start, stop, scale, dy, strip, big, square, columns):
    mean = normalize(big, square, start, stop, 384)
    for i in range(start, stop):
        here = span(i, i + 1)
        y = big[here, 0:384] * lax.rsqrt(1.0 + mean[span(i - start, i - start + 1)]) * scale
        row = ROWS * strip - 2 + i
        inside = (dy + row >= 0) & (dy + row < EXTENT) & (row >= 0) & (row < EXTENT)
        y = jnp.where(inside, y, 0.0)
        before, after = shift_sections(y, 384)
        columns[here, 0:384] = before.astype(BF16)
        columns[here, 384:768] = y.astype(BF16)
        columns[here, 768:1152] = after.astype(BF16)


def third_multiply(start, stop, columns, band_three, big):
    for g in range(2):
        total = None
        for b in range(3):
            for a in range(3):
                lhs = columns[span(start + b, stop + b), 384 * a + 128 * g : 384 * a + 128 * g + 256]
                rhs = band_three[3 * b + a]
                term = dot_nt(lhs, rhs if g else rhs[0:128])
                total = term if total is None else total + term
        if g:
            big[span(start, stop), 128:384] = total
        else:
            big[span(start, stop), 0:128] = total


def third_mask(block):
    lane = iota((SECS, 384), 1)
    column = jnp.where(lane < 320, lane, lane - 64) // C + (BLOCK * block - 1)
    return (column >= 0) & (column < EXTENT)


def third_finish(start, stop, inside, strip, big, middle):
    low = iota((SECS, 128), 1) < 64
    for i in range(start, stop):
        row = ROWS * strip - 1 + i
        y = silu(big[span(i, i + 1), 0:384])
        y = jnp.where(inside & (row >= 0) & (row < EXTENT), y, 0.0)
        before, after = shift_sections(y, 384)
        here = span(i, i + 1)
        middle[here, 0:256] = before[:, 0:256].astype(BF16)
        middle[here, 256:512] = y[:, 0:256].astype(BF16)
        middle[here, 512:768] = after[:, 0:256].astype(BF16)
        middle[here, 768:896] = jnp.where(low, before[:, 256:384], y[:, 256:384]).astype(BF16)
        middle[here, 896:1024] = after[:, 256:384].astype(BF16)


def fourth(start, stop, middle, band_four, out):
    total = None
    for b in range(3):
        term = dot_nt(middle[span(start + b, stop + b), :], band_four[b])
        total = term if total is None else total + term
    for i in range(start, stop):
        out[:, i, :] = total[span(i - start, i - start + 1)]


def layers(
    recv, offsets, gain_one, gain_two, strip, block, band_one, band_two, band_three, band_four,
    stage, lhs, big_one, big_two, big_three, square_one, square_two, level, columns, middle, out,
):
    gather_first(recv, stage, lhs)
    dy, dx = as_column(offsets[0:1, :]), as_column(offsets[1:2, :])
    scale_one, scale_two = first_scale(gain_one, dx, block), second_scale(gain_two, dx, block)
    mask = third_mask(block)

    def one(n):
        first_finish(*FIRST[n : n + 2], scale_one, dy, strip, big_one, square_one, level)

    def two(n):
        second_finish(*SECOND[n : n + 2], scale_two, dy, strip, big_two, square_two, columns)

    def three(n):
        third_finish(*THIRD[n : n + 2], mask, strip, big_three, middle)

    first_multiply(0, lhs, band_one, big_one)
    first_multiply(1, lhs, band_one, big_one)
    one(0)
    second_multiply(*SECOND[0:2], level, band_two, big_two)
    one(1)
    second_multiply(*SECOND[1:3], level, band_two, big_two)
    two(0)
    two(1)
    third_multiply(*THIRD[0:2], columns, band_three, big_three)
    third_multiply(*THIRD[1:3], columns, band_three, big_three)
    three(0)
    three(1)
    fourth(*FOURTH, middle, band_four, out)


def kernel(
    raw_hbm, w_first_hbm, gain_one_hbm, w_second_hbm, gain_two_hbm, offsets_hbm, w_third_hbm,
    w_fourth_hbm, out,
    w_first, gain_one, w_second, gain_two, offsets, w_third, w_fourth, offsets_smem,
    ext, send, recv, band_one, band_two, band_three, band_four, tile, wide, stage, lhs, big_one,
    big_two, big_three, square_one, square_two, level, columns, middle, load_sem, halo_send, halo_recv, pass_send, pass_recv,
):
    me, strip = lax.axis_index("sec"), lax.axis_index("strip")
    up = lax.rem(strip + STRIPS - 1, STRIPS)
    down = lax.rem(strip + 1, STRIPS)

    loads = [
        pltpu.make_async_copy(source, target, load_sem.at[n])
        for n, (source, target) in enumerate(
            (
                (raw_hbm, ext.at[32:64, :]),
                (offsets_hbm, offsets_smem),
                (w_first_hbm, w_first),
                (w_second_hbm, w_second),
                (w_third_hbm, w_third),
                (w_fourth_hbm, w_fourth),
                (gain_one_hbm, gain_one),
                (gain_two_hbm, gain_two),
                (offsets_hbm, offsets),
            )
        )
    ]
    for load in loads:
        load.start()

    barrier = pltpu.get_barrier_semaphore()
    for near in (up, down):
        pl.semaphore_signal(barrier, inc=1, device_id={"strip": near}, device_id_type=MESH_ID)
    for x, z in PEERS:
        peer = peer_at(me, x, z)
        pl.semaphore_signal(barrier, inc=1, device_id={"sec": peer}, device_id_type=MESH_ID)

    for load in loads:
        load.wait()
    pl.semaphore_wait(barrier, SECS + 1)

    halos = []
    for n, (near, start) in enumerate(((down, 0), (up, 64))):
        copy = pltpu.make_async_remote_copy(
            src_ref=ext.at[32:64, :], dst_ref=ext.at[start : start + 32, :],
            send_sem=halo_send.at[n], recv_sem=halo_recv.at[n],
            device_id={"strip": near}, device_id_type=MESH_ID,
        )
        copy.start()
        halos.append(copy)
    build_first(w_first, tile, band_one)
    build_second(w_second, wide, band_two)
    dy, dx = offsets_smem[0, me], offsets_smem[1, me]
    chosen = pick_rows(strip, dy)
    for copy in halos:
        copy.wait_recv()
    cut_windows(dot_nn(chosen, ext[...]), dx, send)

    for x, z in PEERS:
        peer = peer_at(me, x, z)
        pltpu.make_async_remote_copy(
            src_ref=send.at[peer], dst_ref=recv.at[me], send_sem=pass_send, recv_sem=pass_recv,
            device_id={"sec": peer}, device_id_type=MESH_ID,
        ).start()
    recv[me] = send[me]
    build_third(w_third, wide, band_three)
    build_fourth(w_fourth, wide, band_four)
    gain_a, gain_b = build_gain(gain_one, tile), build_gain(gain_two, tile)
    pltpu.make_async_copy(send.at[0 : SECS - 1], recv.at[0 : SECS - 1], pass_recv).wait()
    pltpu.make_async_copy(send.at[0 : SECS - 1], recv.at[0 : SECS - 1], pass_send).wait()
    for copy in halos:
        copy.wait_send()

    layers(
        recv, offsets, gain_a, gain_b, strip, me, band_one, band_two, band_three, band_four,
        stage, lhs, big_one, big_two, big_three, square_one, square_two, level, columns, middle, out,
    )


def shards(raw_image, w_first, gain_one, w_second, gain_two, offsets, w_third, w_fourth):
    hbm = pl.BlockSpec(memory_space=pltpu.HBM)
    result = pl.pallas_call(
        kernel,
        out_shape=jax.ShapeDtypeStruct((SECS, ROWS, C * BLOCK), F32),
        in_specs=[hbm] * 8,
        out_specs=pl.BlockSpec(memory_space=pltpu.VMEM),
        scratch_shapes=[
            pltpu.VMEM((9, C), BF16),
            pltpu.VMEM((1, C), F32),
            pltpu.VMEM((3, C, 96), BF16),
            pltpu.VMEM((1, C), F32),
            pltpu.VMEM((2, SECS), jnp.int32),
            pltpu.VMEM((9, C, 96), BF16),
            pltpu.VMEM((9, C, 96), BF16),
            pltpu.SMEM((2, SECS), jnp.int32),
            pltpu.VMEM((96, RAW), BF16),
            pltpu.VMEM((SECS, 16, 128), BF16),
            pltpu.VMEM((SECS, 16, 128), BF16),
            pltpu.VMEM((2, 256, 512), BF16),
            pltpu.VMEM((2, 256, 768), BF16),
            pltpu.VMEM((9, 256, 256), BF16),
            pltpu.VMEM((3, 256, 1024), BF16),
            pltpu.VMEM((16, 128), F32),
            pltpu.VMEM((C, 256), F32),
            pltpu.VMEM((SECS * 16, 128), F32),
            pltpu.VMEM((352, 256), BF16),
            pltpu.VMEM((704, 512), F32),
            pltpu.VMEM((640, 384), F32),
            pltpu.VMEM((576, 384), F32),
            pltpu.VMEM((704, 512), BF16),
            pltpu.VMEM((640, 384), BF16),
            pltpu.VMEM((704, 512), BF16),
            pltpu.VMEM((640, 1152), BF16),
            pltpu.VMEM((576, 1024), BF16),
            pltpu.SemaphoreType.DMA((9,)),
            pltpu.SemaphoreType.DMA((2,)),
            pltpu.SemaphoreType.DMA((2,)),
            pltpu.SemaphoreType.DMA,
            pltpu.SemaphoreType.DMA,
        ],
        compiler_params=pltpu.CompilerParams(
            collective_id=0, has_side_effects=True, vmem_limit_bytes=48 * 2**20
        ),
        cost_estimate=pl.CostEstimate(flops=10**9, bytes_accessed=2**20, transcendentals=10**6),
    )(
        *[
            pltpu.with_memory_space_constraint(x, pltpu.HBM)
            for x in (
                raw_image.reshape(32, RAW), w_first, gain_one.reshape(1, C), w_second,
                gain_two.reshape(1, C), offsets.T, w_third, w_fourth,
            )
        ]
    )
    return result.reshape(1, SECS, ROWS, C * BLOCK)


def solution(mesh):
    placed = (P("sec", "strip", None), P(), P(), P(), P(), P(), P(), P())
    return jax.shard_map(
        shards, mesh=mesh, in_specs=placed, out_specs=P("sec", None, "strip", None), check_vma=False
    )
```

```python
import jax
import jax.numpy as jnp
from jax import lax
from jax.experimental import pallas as pl
from jax.experimental.pallas import tpu as pltpu
from jax.sharding import PartitionSpec as P

C = 32
SECS = 32
BLOCK = 8
ROWS = 16
EXTENT = 256
RAW = 512
STRIPS = 16

F32, BF16 = jnp.float32, jnp.bfloat16
MESH_ID = pl.DeviceIdType.MESH


PEERS = sorted(
    [(x, z) for x in range(4) for z in range(8) if x or z],
    key=lambda at: -(min(at[0], 4 - at[0]) + min(at[1], 8 - at[1])),
)


def peer_at(me, x, z):
    return lax.rem(me // 8 + x, 4) * 8 + lax.rem(lax.rem(me, 8) + z, 8)


SEND_ORDER = sorted(range(SECS), key=lambda k: (k % 8, k // 8))


def group_of(s):
    return ((s % 8 + 2) % 8) // 4


def slot_of(s):
    x, z, g = s // 8, s % 8, group_of(s)
    return 16 * g + 8 * (x // 2) + (z + 4 * ((x + g) % 2)) % 8


def iota(shape, axis):
    return lax.broadcasted_iota(jnp.int32, shape, axis)


def dot_nn(a, b):
    return jnp.dot(a, b, preferred_element_type=F32)


def dot_nt(a, b):
    return lax.dot_general(a, b, (((1,), (1,)), ((), ())), preferred_element_type=F32)


def silu(u):
    half = 0.5 * u
    return half + half * jnp.tanh(half)


def widen(ref, small, rows, count):
    ref[0:rows, :] = jnp.zeros((rows, 128), F32)
    ref[0:rows, 0:count] = small.astype(F32)
    return ref[0:rows, :]


def build_first(w_first, tile, band_one):
    base = widen(tile, w_first[...], 9, C)
    base = base + pltpu.roll(base, 32, 1)
    base = base + pltpu.roll(base, 64, 1)
    taps = jnp.concatenate([base] * 4, axis=1)
    lane = iota((32, 512), 1)
    column = 6 * (lane // 256) + (lane % 256) // 32
    shift = iota((32, 512), 0) - 1 - 2 * column
    band_one[...] = jnp.zeros(band_one.shape, BF16)
    for a, start in ((0, 32), (1, 128), (2, 160)):
        block = jnp.zeros((32, 512), F32)
        for b in range(3):
            block = jnp.where(shift == b, taps[3 * a + b : 3 * a + b + 1, :], block)
        for half in range(2):
            band_one[half, start + 64 * half : start + 64 * half + 32, :] = block.astype(BF16)


def build_gain(gain, tile):
    base = widen(tile, gain[...], 1, C)
    base = base + pltpu.roll(base, 32, 1)
    return base + pltpu.roll(base, 64, 1)


def build_second(w_second, wide, band_two):
    wide[...] = jnp.zeros(wide.shape, F32)
    for a in range(3):
        wide[:, 0:96] = w_second[a].astype(F32)
        base = wide[:, 0:256]
        for x in range(6):
            block = pltpu.roll(base, 32 * x, 1).astype(BF16) if x else base.astype(BF16)
            band_two[0, 32 * x : 32 * x + 32, 256 * a : 256 * a + 256] = block
            band_two[1, 64 + 32 * x : 96 + 32 * x, 256 * a : 256 * a + 256] = block
        band_two[0, 192:256, 256 * a : 256 * a + 256] = jnp.zeros((64, 256), BF16)
        band_two[1, 0:64, 256 * a : 256 * a + 256] = jnp.zeros((64, 256), BF16)


def tap_base(weight, wide, a, b):
    lane = iota((C, 128), 1)
    total = jnp.zeros((C, 128), F32)
    for e in range(3):
        wide[:, 0:96] = weight[3 * b + e].astype(F32)
        part = wide[:, 0:128]
        turn = (32 * (e - a)) % 128
        part = pltpu.roll(part, turn, 1) if turn else part
        total = jnp.where(lane // 32 == e, part, total)
    return jnp.concatenate([total, jnp.zeros((C, 256), F32)], axis=1)


def build_third(w_third, wide, band_three):
    wide[...] = jnp.zeros(wide.shape, F32)
    for a in range(3):
        for b in range(3):
            base = tap_base(w_third, wide, a, b)[:, 0:256]
            where = 3 * b + a
            for x in range(6):
                block = pltpu.roll(base, 32 * x, 1).astype(BF16) if x else base.astype(BF16)
                band_three[where, 32 * x : 32 * x + 32, :] = block
                if x >= 4:
                    band_three[where, 64 + 32 * x : 96 + 32 * x, :] = block


def build_fourth(w_fourth, wide, band_four):
    wide[...] = jnp.zeros(wide.shape, F32)
    row = iota((256, 256), 0)
    order = jnp.where(iota((256, 256), 1) == (row % BLOCK) * C + row // BLOCK, 1.0, 0.0).astype(BF16)
    for b in range(3):
        edges = []
        for a in range(3):
            base = tap_base(w_fourth, wide, a, b)
            stack = [
                (pltpu.roll(base, 32 * x, 1) if x else base).astype(BF16) for x in range(BLOCK)
            ]
            band = dot_nn(order, jnp.concatenate(stack, axis=0))
            band_four[b, :, 256 * a : 256 * a + 256] = band[:, 0:256].astype(BF16)
            edges.append(band[:, 256:384])
        band_four[b, :, 768:896] = (edges[0] + pltpu.roll(edges[1], 64, 1)).astype(BF16)
        band_four[b, :, 896:1024] = edges[2].astype(BF16)


def pick_rows(strip, dy):
    m = iota((64, 96), 0)
    half, parity, q = m // 32, (m // 16) % 2, m % 16
    row = 2 * (dy - 4 + 11 * half + q) + parity
    inside = (row + 32 * strip >= 0) & (row + 32 * strip < RAW)
    return jnp.where(inside & (iota((64, 96), 1) - 32 == row), 1.0, 0.0).astype(BF16)


def cut_windows(rows, dx, send, start=lambda k: None):
    padded = jnp.concatenate([rows, jnp.zeros((64, 128), F32)], axis=1)
    shifted = pltpu.roll(padded, lax.rem(648 - 2 * dx, 640), 1)
    lane = iota((16, 128), 1)
    low = (lane // 64) == 0
    even = (lane // 32) % 2 == 0
    for odd in range(2):
        view = pltpu.roll(shifted, 624, 1) if odd else shifted
        for tile in range(4):
            parts = [view[16 * p : 16 * p + 16, 128 * tile : 128 * tile + 128] for p in range(4)]
            for m1 in range(2):
                pair = []
                for h0 in range(2):
                    first, second = parts[h0], parts[2 + h0]
                    if m1 == 0:
                        pair.append(jnp.where(low, first, pltpu.roll(second, 64, 1)))
                    else:
                        pair.append(jnp.where(low, pltpu.roll(first, 64, 1), second))
                group = 4 * tile + 2 * m1
                here = jnp.where(even, pair[0], pltpu.roll(pair[1], 32, 1))
                then = jnp.where(even, pltpu.roll(pair[0], 96, 1), pair[1])
                send[2 * group + odd] = here.astype(BF16)
                send[2 * (group + 1) + odd] = then.astype(BF16)
        for k in SEND_ORDER[:4] if odd == 0 else SEND_ORDER[4:]:
            start(k)


def by_slot(row):
    same = iota((SECS, SECS), 0) == slot_of(iota((SECS, SECS), 1))
    return jnp.sum(jnp.where(same, row.astype(F32), 0.0), axis=1, keepdims=True).astype(jnp.int32)


THIRD, FOURTH = (0, 9, 18), (0, 16)
HALF = SECS // 2


def span(start, stop):
    return slice(32 * start, 32 * stop)


def few(start, stop):
    return slice(HALF * start, HALF * stop)


def gather_first(recv, g, stage, lhs):
    stage[g] = recv[few(g, g + 1)].reshape(HALF * 16, 128).astype(F32)
    for q in range(12):
        piece = stage[g, pl.ds(q, HALF, stride=16), :].astype(BF16)
        if q < 11:
            lhs[g, few(q, q + 1), 0:128] = piece
        if q > 0:
            lhs[g, few(q - 1, q), 128:256] = piece


def normalize(big, square, g, count, lanes):
    for i in range(count):
        v = silu(big[g, few(i, i + 1), :])
        big[g, few(i, i + 1), :] = v
        square[g, few(i, i + 1), :] = (v * v).astype(BF16)
    same = iota((256, 256), 0) // C == iota((256, 256), 1) // C
    spread = jnp.where(same, 1.0 / C, 0.0).astype(BF16)
    parts = []
    for low in range(0, lanes, 256):
        wide = min(256, lanes - low)
        parts.append(dot_nn(square[g, :, low : low + wide], spread[0:wide, 0:wide]))
    return jnp.concatenate(parts, axis=1)


def shift_sections(y, wide_lanes):
    s = iota((SECS, wide_lanes), 0)
    before = jnp.where(s == 0, 0.0, pltpu.roll(y, 1, 0))
    after = jnp.where(s == SECS - 1, 0.0, pltpu.roll(y, SECS - 1, 0))
    return before, after


def first_multiply(g, lhs, band_one, big):
    for half in range(2):
        big[g, few(11 * half, 11 * half + 11), :] = dot_nn(lhs[g], band_one[half])


def first_scale(gain, dx, block):
    lane = iota((HALF, 512), 1)
    column = 6 * (lane // 256) + (lane % 256) // 32
    inside = column + dx + (BLOCK * block - 3) < EXTENT
    return jnp.where(inside, jnp.concatenate([gain] * 4, axis=1), 0.0)


def first_finish(g, scale, dy, strip, big, square, level):
    mean = normalize(big, square, g, 22, 512)
    for i in range(22):
        here = few(i, i + 1)
        y = big[g, here, :] * lax.rsqrt(1.0 + mean[here]) * scale
        y = jnp.where(dy + (ROWS * strip - 3 + i) < EXTENT, y, 0.0)
        level[g, here, :] = y.astype(BF16)


def second_multiply(g, level, band_two, big):
    parts = []
    for side in range(2):
        lhs = jnp.concatenate(
            [level[g, few(a, a + 20), 256 * side : 256 * side + 256] for a in range(3)], axis=1
        )
        parts.append(dot_nt(lhs, band_two[side]))
    big[g, :, 0:128] = parts[0][:, 0:128]
    big[g, :, 128:256] = parts[0][:, 128:256] + parts[1][:, 0:128]
    big[g, :, 256:384] = parts[1][:, 128:256]


def second_scale(gain, dx, block):
    placed = iota((HALF, 384), 1) // C + (BLOCK * block - 2)
    inside = (placed >= 0) & (placed < EXTENT) & (placed + dx >= 0) & (placed + dx < EXTENT)
    return jnp.where(inside, jnp.concatenate([gain] * 3, axis=1), 0.0)


def second_finish(g, scale, dy, strip, big, square):
    mean = normalize(big, square, g, 20, 384)
    for i in range(20):
        here = few(i, i + 1)
        y = big[g, here, :] * lax.rsqrt(1.0 + mean[here]) * scale
        row = ROWS * strip - 2 + i
        inside = (dy + row >= 0) & (dy + row < EXTENT) & (row >= 0) & (row < EXTENT)
        big[g, here, :] = jnp.where(inside, y, 0.0)


def merge(big, columns):
    pos = iota((8, 384), 0)
    outer = (pos < 2) | (pos >= 6)
    for i in range(20):
        tiles = []
        for t in range(2):
            at = slice(HALF * i + 8 * t, HALF * i + 8 * t + 8)
            a, b = big[0, at, :], big[1, at, :]
            tiles.append(jnp.where(outer, a, pltpu.roll(b, 4, 0)))
            tiles.append(jnp.where(outer, pltpu.roll(a, 4, 0), b))
        y = jnp.concatenate(tiles, axis=0)
        before, after = shift_sections(y, 384)
        here = span(i, i + 1)
        columns[here, 0:384] = before.astype(BF16)
        columns[here, 384:768] = y.astype(BF16)
        columns[here, 768:1152] = after.astype(BF16)


def third_multiply(start, stop, columns, band_three, big):
    for g in range(2):
        total = None
        for b in range(3):
            for a in range(3):
                lhs = columns[span(start + b, stop + b), 384 * a + 128 * g : 384 * a + 128 * g + 256]
                rhs = band_three[3 * b + a]
                term = dot_nt(lhs, rhs if g else rhs[0:128])
                total = term if total is None else total + term
        if g:
            big[span(start, stop), 128:384] = total
        else:
            big[span(start, stop), 0:128] = total


def third_mask(block):
    lane = iota((SECS, 384), 1)
    column = jnp.where(lane < 320, lane, lane - 64) // C + (BLOCK * block - 1)
    return (column >= 0) & (column < EXTENT)


def third_finish(start, stop, inside, strip, big, middle):
    low = iota((SECS, 128), 1) < 64
    for i in range(start, stop):
        row = ROWS * strip - 1 + i
        y = silu(big[span(i, i + 1), 0:384])
        y = jnp.where(inside & (row >= 0) & (row < EXTENT), y, 0.0)
        before, after = shift_sections(y, 384)
        here = span(i, i + 1)
        middle[here, 0:256] = before[:, 0:256].astype(BF16)
        middle[here, 256:512] = y[:, 0:256].astype(BF16)
        middle[here, 512:768] = after[:, 0:256].astype(BF16)
        middle[here, 768:896] = jnp.where(low, before[:, 256:384], y[:, 256:384]).astype(BF16)
        middle[here, 896:1024] = after[:, 256:384].astype(BF16)


def fourth(start, stop, middle, band_four, out):
    total = None
    for b in range(3):
        term = dot_nt(middle[span(start + b, stop + b), :], band_four[b])
        total = term if total is None else total + term
    for i in range(start, stop):
        out[:, i, :] = total[span(i - start, i - start + 1)]


def layers(
    arrived, recv, offsets, gain_one, gain_two, strip, block, band_one, band_two, band_three,
    band_four, stage, lhs, big_one, big_two, big_three, square_one, square_two, level, columns,
    middle, out,
):
    dys, dxs = by_slot(offsets[0:1, :]), by_slot(offsets[1:2, :])
    mask = third_mask(block)
    for g in range(2):
        dy, dx = dys[few(g, g + 1)], dxs[few(g, g + 1)]
        scale_one, scale_two = first_scale(gain_one, dx, block), second_scale(gain_two, dx, block)
        arrived(g)
        gather_first(recv, g, stage, lhs)
        first_multiply(g, lhs, band_one, big_one)
        first_finish(g, scale_one, dy, strip, big_one, square_one, level)
        second_multiply(g, level, band_two, big_two)
        second_finish(g, scale_two, dy, strip, big_two, square_two)
    merge(big_two, columns)
    third_multiply(*THIRD[0:2], columns, band_three, big_three)
    third_multiply(*THIRD[1:3], columns, band_three, big_three)
    third_finish(*THIRD[0:2], mask, strip, big_three, middle)
    third_finish(*THIRD[1:3], mask, strip, big_three, middle)
    fourth(*FOURTH, middle, band_four, out)


def kernel(
    raw_hbm, w_first_hbm, gain_one_hbm, w_second_hbm, gain_two_hbm, offsets_hbm, w_third_hbm,
    w_fourth_hbm, out,
    w_first, gain_one, w_second, gain_two, offsets, w_third, w_fourth, offsets_smem,
    ext, send, recv, band_one, band_two, band_three, band_four, tile, wide, stage, lhs, big_one,
    big_two, big_three, square_one, square_two, level, columns, middle, load_sem, halo_send, halo_recv, pass_send, pass_recv,
):
    me, strip = lax.axis_index("sec"), lax.axis_index("strip")
    up = lax.rem(strip + STRIPS - 1, STRIPS)
    down = lax.rem(strip + 1, STRIPS)

    loads = [
        pltpu.make_async_copy(source, target, load_sem.at[n])
        for n, (source, target) in enumerate(
            (
                (raw_hbm, ext.at[32:64, :]),
                (offsets_hbm, offsets_smem),
                (w_first_hbm, w_first),
                (w_second_hbm, w_second),
                (w_third_hbm, w_third),
                (w_fourth_hbm, w_fourth),
                (gain_one_hbm, gain_one),
                (gain_two_hbm, gain_two),
                (offsets_hbm, offsets),
            )
        )
    ]
    for load in loads:
        load.start()

    barrier = pltpu.get_barrier_semaphore()
    for near in (up, down):
        pl.semaphore_signal(barrier, inc=1, device_id={"strip": near}, device_id_type=MESH_ID)
    for x, z in PEERS:
        peer = peer_at(me, x, z)
        pl.semaphore_signal(barrier, inc=1, device_id={"sec": peer}, device_id_type=MESH_ID)

    for load in loads:
        load.wait()
    pl.semaphore_wait(barrier, SECS + 1)

    halos = []
    for n, (near, start) in enumerate(((down, 0), (up, 64))):
        copy = pltpu.make_async_remote_copy(
            src_ref=ext.at[32:64, :], dst_ref=ext.at[start : start + 32, :],
            send_sem=halo_send.at[n], recv_sem=halo_recv.at[n],
            device_id={"strip": near}, device_id_type=MESH_ID,
        )
        copy.start()
        halos.append(copy)
    build_first(w_first, tile, band_one)
    build_second(w_second, wide, band_two)
    dy, dx = offsets_smem[0, me], offsets_smem[1, me]
    chosen = pick_rows(strip, dy)
    for copy in halos:
        copy.wait_recv()
    slot, group = slot_of(me), group_of(me)

    def start(k):
        @pl.when(me != k)
        def _():
            pltpu.make_async_remote_copy(
                src_ref=send.at[k], dst_ref=recv.at[slot], send_sem=pass_send,
                recv_sem=pass_recv.at[group], device_id={"sec": k}, device_id_type=MESH_ID,
            ).start()

    cut_windows(dot_nn(chosen, ext[...]), dx, send, start)
    pltpu.make_async_copy(send.at[me], recv.at[slot], pass_recv.at[group]).start()
    build_third(w_third, wide, band_three)
    build_fourth(w_fourth, wide, band_four)
    gain_a, gain_b = build_gain(gain_one, tile), build_gain(gain_two, tile)

    def arrived(g):
        pltpu.make_async_copy(
            send.at[0:HALF], recv.at[HALF * g : HALF * g + HALF], pass_recv.at[g]
        ).wait()

    layers(
        arrived, recv, offsets, gain_a, gain_b, strip, me, band_one, band_two, band_three,
        band_four, stage, lhs, big_one, big_two, big_three, square_one, square_two, level, columns,
        middle, out,
    )
    pltpu.make_async_copy(send.at[0 : SECS - 1], recv.at[0 : SECS - 1], pass_send).wait()
    for copy in halos:
        copy.wait_send()


def shards(raw_image, w_first, gain_one, w_second, gain_two, offsets, w_third, w_fourth):
    hbm = pl.BlockSpec(memory_space=pltpu.HBM)
    result = pl.pallas_call(
        kernel,
        out_shape=jax.ShapeDtypeStruct((SECS, ROWS, C * BLOCK), F32),
        in_specs=[hbm] * 8,
        out_specs=pl.BlockSpec(memory_space=pltpu.VMEM),
        scratch_shapes=[
            pltpu.VMEM((9, C), BF16),
            pltpu.VMEM((1, C), F32),
            pltpu.VMEM((3, C, 96), BF16),
            pltpu.VMEM((1, C), F32),
            pltpu.VMEM((2, SECS), jnp.int32),
            pltpu.VMEM((9, C, 96), BF16),
            pltpu.VMEM((9, C, 96), BF16),
            pltpu.SMEM((2, SECS), jnp.int32),
            pltpu.VMEM((96, RAW), BF16),
            pltpu.VMEM((SECS, 16, 128), BF16),
            pltpu.VMEM((SECS, 16, 128), BF16),
            pltpu.VMEM((2, 256, 512), BF16),
            pltpu.VMEM((2, 256, 768), BF16),
            pltpu.VMEM((9, 256, 256), BF16),
            pltpu.VMEM((3, 256, 1024), BF16),
            pltpu.VMEM((16, 128), F32),
            pltpu.VMEM((C, 256), F32),
            pltpu.VMEM((2, HALF * 16, 128), F32),
            pltpu.VMEM((2, 11 * HALF, 256), BF16),
            pltpu.VMEM((2, 22 * HALF, 512), F32),
            pltpu.VMEM((2, 20 * HALF, 384), F32),
            pltpu.VMEM((576, 384), F32),
            pltpu.VMEM((2, 22 * HALF, 512), BF16),
            pltpu.VMEM((2, 20 * HALF, 384), BF16),
            pltpu.VMEM((2, 22 * HALF, 512), BF16),
            pltpu.VMEM((640, 1152), BF16),
            pltpu.VMEM((576, 1024), BF16),
            pltpu.SemaphoreType.DMA((9,)),
            pltpu.SemaphoreType.DMA((2,)),
            pltpu.SemaphoreType.DMA((2,)),
            pltpu.SemaphoreType.DMA,
            pltpu.SemaphoreType.DMA((2,)),
        ],
        compiler_params=pltpu.CompilerParams(
            collective_id=0, has_side_effects=True, vmem_limit_bytes=48 * 2**20
        ),
        cost_estimate=pl.CostEstimate(flops=10**9, bytes_accessed=2**20, transcendentals=10**6),
    )(
        *[
            pltpu.with_memory_space_constraint(x, pltpu.HBM)
            for x in (
                raw_image.reshape(32, RAW), w_first, gain_one.reshape(1, C), w_second,
                gain_two.reshape(1, C), offsets.T, w_third, w_fourth,
            )
        ]
    )
    return result.reshape(1, SECS, ROWS, C * BLOCK)


def solution(mesh):
    placed = (P("sec", "strip", None), P(), P(), P(), P(), P(), P(), P())
    return jax.shard_map(
        shards, mesh=mesh, in_specs=placed, out_specs=P("sec", None, "strip", None), check_vma=False
    )
```

```python
import jax
import jax.numpy as jnp
from jax import lax
from jax.experimental import pallas as pl
from jax.experimental.pallas import tpu as pltpu
from jax.sharding import PartitionSpec as P

C = 32
SECS = 32
BLOCK = 8
ROWS = 16
EXTENT = 256
RAW = 512
STRIPS = 16

F32, BF16 = jnp.float32, jnp.bfloat16
MESH_ID = pl.DeviceIdType.MESH


PEERS = sorted(
    [(x, z) for x in range(4) for z in range(8) if x or z],
    key=lambda at: -(min(at[0], 4 - at[0]) + min(at[1], 8 - at[1])),
)


def peer_at(me, x, z):
    return lax.rem(me // 8 + x, 4) * 8 + lax.rem(lax.rem(me, 8) + z, 8)


SEND_ORDER = sorted(range(SECS), key=lambda k: (k % 8, k // 8))


def group_of(s):
    return ((s % 8 + 2) % 8) // 4


def slot_of(s):
    x, z, g = s // 8, s % 8, group_of(s)
    return 16 * g + 8 * (x // 2) + (z + 4 * ((x + g) % 2)) % 8


def iota(shape, axis):
    return lax.broadcasted_iota(jnp.int32, shape, axis)


def dot_nn(a, b):
    return jnp.dot(a, b, preferred_element_type=F32)


def dot_nt(a, b):
    return lax.dot_general(a, b, (((1,), (1,)), ((), ())), preferred_element_type=F32)


def silu(u):
    half = 0.5 * u
    return half + half * jnp.tanh(half)


def widen(ref, small, rows, count):
    ref[0:rows, :] = jnp.zeros((rows, 128), F32)
    ref[0:rows, 0:count] = small.astype(F32)
    return ref[0:rows, :]


def build_first(w_first, tile, band_one):
    base = widen(tile, w_first[...], 9, C)
    base = base + pltpu.roll(base, 32, 1)
    base = base + pltpu.roll(base, 64, 1)
    taps = jnp.concatenate([base] * 4, axis=1)
    lane = iota((32, 512), 1)
    column = 6 * (lane // 256) + (lane % 256) // 32
    shift = iota((32, 512), 0) - 1 - 2 * column
    band_one[...] = jnp.zeros(band_one.shape, BF16)
    for a, start in ((0, 32), (1, 128), (2, 160)):
        block = jnp.zeros((32, 512), F32)
        for b in range(3):
            block = jnp.where(shift == b, taps[3 * a + b : 3 * a + b + 1, :], block)
        for half in range(2):
            band_one[half, start + 64 * half : start + 64 * half + 32, :] = block.astype(BF16)


def build_gain(gain, tile):
    base = widen(tile, gain[...], 1, C)
    base = base + pltpu.roll(base, 32, 1)
    return base + pltpu.roll(base, 64, 1)


def build_second(w_second, wide, band_two):
    wide[...] = jnp.zeros(wide.shape, F32)
    for a in range(3):
        wide[:, 0:96] = w_second[a].astype(F32)
        base = wide[:, 0:256]
        for x in range(6):
            block = pltpu.roll(base, 32 * x, 1).astype(BF16) if x else base.astype(BF16)
            band_two[0, 32 * x : 32 * x + 32, 256 * a : 256 * a + 256] = block
            band_two[1, 64 + 32 * x : 96 + 32 * x, 256 * a : 256 * a + 256] = block
        band_two[0, 192:256, 256 * a : 256 * a + 256] = jnp.zeros((64, 256), BF16)
        band_two[1, 0:64, 256 * a : 256 * a + 256] = jnp.zeros((64, 256), BF16)


def tap_base(weight, wide, a, b):
    lane = iota((C, 128), 1)
    total = jnp.zeros((C, 128), F32)
    for e in range(3):
        wide[:, 0:96] = weight[3 * b + e].astype(F32)
        part = wide[:, 0:128]
        turn = (32 * (e - a)) % 128
        part = pltpu.roll(part, turn, 1) if turn else part
        total = jnp.where(lane // 32 == e, part, total)
    return jnp.concatenate([total, jnp.zeros((C, 256), F32)], axis=1)


def build_third(w_third, wide, band_three):
    wide[...] = jnp.zeros(wide.shape, F32)
    for a in range(3):
        for b in range(3):
            base = tap_base(w_third, wide, a, b)[:, 0:256]
            where = 3 * b + a
            for x in range(6):
                block = pltpu.roll(base, 32 * x, 1).astype(BF16) if x else base.astype(BF16)
                band_three[where, 32 * x : 32 * x + 32, :] = block
                if x >= 4:
                    band_three[where, 64 + 32 * x : 96 + 32 * x, :] = block


def build_fourth(w_fourth, wide, band_four):
    wide[...] = jnp.zeros(wide.shape, F32)
    row = iota((256, 256), 0)
    order = jnp.where(iota((256, 256), 1) == (row % BLOCK) * C + row // BLOCK, 1.0, 0.0).astype(BF16)
    for b in range(3):
        edges = []
        for a in range(3):
            base = tap_base(w_fourth, wide, a, b)
            stack = [
                (pltpu.roll(base, 32 * x, 1) if x else base).astype(BF16) for x in range(BLOCK)
            ]
            band = dot_nn(order, jnp.concatenate(stack, axis=0))
            band_four[b, :, 256 * a : 256 * a + 256] = band[:, 0:256].astype(BF16)
            edges.append(band[:, 256:384])
        band_four[b, :, 768:896] = (edges[0] + pltpu.roll(edges[1], 64, 1)).astype(BF16)
        band_four[b, :, 896:1024] = edges[2].astype(BF16)


def pick_rows(strip, dy):
    m = iota((64, 96), 0)
    half, parity, q = m // 32, (m // 16) % 2, m % 16
    row = 2 * (dy - 4 + 11 * half + q) + parity
    inside = (row + 32 * strip >= 0) & (row + 32 * strip < RAW)
    return jnp.where(inside & (iota((64, 96), 1) - 32 == row), 1.0, 0.0).astype(BF16)


def shift_columns(rows, dx):
    padded = jnp.concatenate([rows.astype(F32), jnp.zeros((32, 128), F32)], axis=1)
    return pltpu.roll(padded, lax.rem(648 - 2 * dx, 640), 1).astype(BF16)


def cut_windows(shifted, send, start=lambda k: None):
    lane = iota((16, 128), 1)
    low = (lane // 64) == 0
    even = (lane // 32) % 2 == 0
    for odd in range(2):
        view = pltpu.roll(shifted, 624, 1) if odd else shifted
        for tile in range(4):
            parts = [view[16 * p : 16 * p + 16, 128 * tile : 128 * tile + 128] for p in range(4)]
            for m1 in range(2):
                pair = []
                for h0 in range(2):
                    first, second = parts[h0], parts[2 + h0]
                    if m1 == 0:
                        pair.append(jnp.where(low, first, pltpu.roll(second, 64, 1)))
                    else:
                        pair.append(jnp.where(low, pltpu.roll(first, 64, 1), second))
                group = 4 * tile + 2 * m1
                here = jnp.where(even, pair[0], pltpu.roll(pair[1], 32, 1))
                then = jnp.where(even, pltpu.roll(pair[0], 96, 1), pair[1])
                send[2 * group + odd] = here.astype(BF16)
                send[2 * (group + 1) + odd] = then.astype(BF16)
        for k in SEND_ORDER[:4] if odd == 0 else SEND_ORDER[4:]:
            start(k)


def by_slot(row):
    same = iota((SECS, SECS), 0) == slot_of(iota((SECS, SECS), 1))
    return jnp.sum(jnp.where(same, row.astype(F32), 0.0), axis=1, keepdims=True).astype(jnp.int32)


THIRD, FOURTH = (0, 9, 18), (0, 16)
HALF = SECS // 2


def span(start, stop):
    return slice(32 * start, 32 * stop)


def few(start, stop):
    return slice(HALF * start, HALF * stop)


def gather_first(recv, g, stage, lhs):
    stage[g] = recv[few(g, g + 1)].reshape(HALF * 16, 128).astype(F32)
    for q in range(12):
        piece = stage[g, pl.ds(q, HALF, stride=16), :].astype(BF16)
        if q < 11:
            lhs[g, few(q, q + 1), 0:128] = piece
        if q > 0:
            lhs[g, few(q - 1, q), 128:256] = piece


def normalize(big, square, g, count, lanes):
    for i in range(count):
        v = silu(big[g, few(i, i + 1), :])
        big[g, few(i, i + 1), :] = v
        square[g, few(i, i + 1), :] = (v * v).astype(BF16)
    same = iota((256, 256), 0) // C == iota((256, 256), 1) // C
    spread = jnp.where(same, 1.0 / C, 0.0).astype(BF16)
    parts = []
    for low in range(0, lanes, 256):
        wide = min(256, lanes - low)
        parts.append(dot_nn(square[g, :, low : low + wide], spread[0:wide, 0:wide]))
    return jnp.concatenate(parts, axis=1)


def shift_sections(y, wide_lanes):
    s = iota((SECS, wide_lanes), 0)
    before = jnp.where(s == 0, 0.0, pltpu.roll(y, 1, 0))
    after = jnp.where(s == SECS - 1, 0.0, pltpu.roll(y, SECS - 1, 0))
    return before, after


def first_multiply(g, lhs, band_one, big):
    for half in range(2):
        big[g, few(11 * half, 11 * half + 11), :] = dot_nn(lhs[g], band_one[half])


def first_scale(gain, dx, block):
    lane = iota((HALF, 512), 1)
    column = 6 * (lane // 256) + (lane % 256) // 32
    inside = column + dx + (BLOCK * block - 3) < EXTENT
    return jnp.where(inside, jnp.concatenate([gain] * 4, axis=1), 0.0)


def first_finish(g, scale, dy, strip, big, square, level):
    mean = normalize(big, square, g, 22, 512)
    for i in range(22):
        here = few(i, i + 1)
        y = big[g, here, :] * lax.rsqrt(1.0 + mean[here]) * scale
        y = jnp.where(dy + (ROWS * strip - 3 + i) < EXTENT, y, 0.0)
        level[g, here, :] = y.astype(BF16)


def second_multiply(g, level, band_two, big):
    parts = []
    for side in range(2):
        lhs = jnp.concatenate(
            [level[g, few(a, a + 20), 256 * side : 256 * side + 256] for a in range(3)], axis=1
        )
        parts.append(dot_nt(lhs, band_two[side]))
    big[g, :, 0:128] = parts[0][:, 0:128]
    big[g, :, 128:256] = parts[0][:, 128:256] + parts[1][:, 0:128]
    big[g, :, 256:384] = parts[1][:, 128:256]


def second_scale(gain, dx, block):
    placed = iota((HALF, 384), 1) // C + (BLOCK * block - 2)
    inside = (placed >= 0) & (placed < EXTENT) & (placed + dx >= 0) & (placed + dx < EXTENT)
    return jnp.where(inside, jnp.concatenate([gain] * 3, axis=1), 0.0)


def second_finish(g, scale, dy, strip, big, square):
    mean = normalize(big, square, g, 20, 384)
    for i in range(20):
        here = few(i, i + 1)
        y = big[g, here, :] * lax.rsqrt(1.0 + mean[here]) * scale
        row = ROWS * strip - 2 + i
        inside = (dy + row >= 0) & (dy + row < EXTENT) & (row >= 0) & (row < EXTENT)
        big[g, here, :] = jnp.where(inside, y, 0.0)


def merge(big, columns):
    pos = iota((8, 384), 0)
    outer = (pos < 2) | (pos >= 6)
    for i in range(20):
        tiles = []
        for t in range(2):
            at = slice(HALF * i + 8 * t, HALF * i + 8 * t + 8)
            a, b = big[0, at, :], big[1, at, :]
            tiles.append(jnp.where(outer, a, pltpu.roll(b, 4, 0)))
            tiles.append(jnp.where(outer, pltpu.roll(a, 4, 0), b))
        y = jnp.concatenate(tiles, axis=0)
        before, after = shift_sections(y, 384)
        here = span(i, i + 1)
        columns[here, 0:384] = before.astype(BF16)
        columns[here, 384:768] = y.astype(BF16)
        columns[here, 768:1152] = after.astype(BF16)


def third_multiply(start, stop, columns, band_three, big):
    for g in range(2):
        total = None
        for b in range(3):
            for a in range(3):
                lhs = columns[span(start + b, stop + b), 384 * a + 128 * g : 384 * a + 128 * g + 256]
                rhs = band_three[3 * b + a]
                term = dot_nt(lhs, rhs if g else rhs[0:128])
                total = term if total is None else total + term
        if g:
            big[span(start, stop), 128:384] = total
        else:
            big[span(start, stop), 0:128] = total


def third_mask(block):
    lane = iota((SECS, 384), 1)
    column = jnp.where(lane < 320, lane, lane - 64) // C + (BLOCK * block - 1)
    return (column >= 0) & (column < EXTENT)


def third_finish(start, stop, inside, strip, big, middle):
    low = iota((SECS, 128), 1) < 64
    for i in range(start, stop):
        row = ROWS * strip - 1 + i
        y = silu(big[span(i, i + 1), 0:384])
        y = jnp.where(inside & (row >= 0) & (row < EXTENT), y, 0.0)
        before, after = shift_sections(y, 384)
        here = span(i, i + 1)
        middle[here, 0:256] = before[:, 0:256].astype(BF16)
        middle[here, 256:512] = y[:, 0:256].astype(BF16)
        middle[here, 512:768] = after[:, 0:256].astype(BF16)
        middle[here, 768:896] = jnp.where(low, before[:, 256:384], y[:, 256:384]).astype(BF16)
        middle[here, 896:1024] = after[:, 256:384].astype(BF16)


def fourth(start, stop, middle, band_four, out):
    total = None
    for b in range(3):
        term = dot_nt(middle[span(start + b, stop + b), :], band_four[b])
        total = term if total is None else total + term
    for i in range(start, stop):
        out[:, i, :] = total[span(i - start, i - start + 1)]


def layers(
    arrived, recv, offsets, gain_one, gain_two, strip, block, band_one, band_two, band_three,
    band_four, stage, lhs, big_one, big_two, big_three, square_one, square_two, level, columns,
    middle, out,
):
    dys, dxs = by_slot(offsets[0:1, :]), by_slot(offsets[1:2, :])
    mask = third_mask(block)
    for g in range(2):
        dy, dx = dys[few(g, g + 1)], dxs[few(g, g + 1)]
        scale_one, scale_two = first_scale(gain_one, dx, block), second_scale(gain_two, dx, block)
        arrived(g)
        gather_first(recv, g, stage, lhs)
        first_multiply(g, lhs, band_one, big_one)
        first_finish(g, scale_one, dy, strip, big_one, square_one, level)
        second_multiply(g, level, band_two, big_two)
        second_finish(g, scale_two, dy, strip, big_two, square_two)
    merge(big_two, columns)
    third_multiply(*THIRD[0:2], columns, band_three, big_three)
    third_multiply(*THIRD[1:3], columns, band_three, big_three)
    third_finish(*THIRD[0:2], mask, strip, big_three, middle)
    third_finish(*THIRD[1:3], mask, strip, big_three, middle)
    fourth(*FOURTH, middle, band_four, out)


def kernel(
    raw_hbm, w_first_hbm, gain_one_hbm, w_second_hbm, gain_two_hbm, offsets_hbm, w_third_hbm,
    w_fourth_hbm, out,
    w_first, gain_one, w_second, gain_two, offsets, w_third, w_fourth, offsets_smem,
    raw, ext, send, recv, band_one, band_two, band_three, band_four, tile, wide, stage, lhs, big_one,
    big_two, big_three, square_one, square_two, level, columns, middle, load_sem, halo_send, halo_recv, pass_send, pass_recv,
):
    me, strip = lax.axis_index("sec"), lax.axis_index("strip")
    up = lax.rem(strip + STRIPS - 1, STRIPS)
    down = lax.rem(strip + 1, STRIPS)

    loads = [
        pltpu.make_async_copy(source, target, load_sem.at[n])
        for n, (source, target) in enumerate(
            (
                (raw_hbm, raw),
                (offsets_hbm, offsets_smem),
                (w_first_hbm, w_first),
                (w_second_hbm, w_second),
                (w_third_hbm, w_third),
                (w_fourth_hbm, w_fourth),
                (gain_one_hbm, gain_one),
                (gain_two_hbm, gain_two),
                (offsets_hbm, offsets),
            )
        )
    ]
    for load in loads:
        load.start()

    barrier = pltpu.get_barrier_semaphore()
    for near in (up, down):
        pl.semaphore_signal(barrier, inc=1, device_id={"strip": near}, device_id_type=MESH_ID)
    for x, z in PEERS:
        peer = peer_at(me, x, z)
        pl.semaphore_signal(barrier, inc=1, device_id={"sec": peer}, device_id_type=MESH_ID)

    for load in loads:
        load.wait()
    dy, dx = offsets_smem[0, me], offsets_smem[1, me]
    ext[32:64, :] = shift_columns(raw[...], dx)
    pl.semaphore_wait(barrier, SECS + 1)

    halos = []
    for n, (near, start) in enumerate(((down, 0), (up, 64))):
        copy = pltpu.make_async_remote_copy(
            src_ref=ext.at[32:64, :], dst_ref=ext.at[start : start + 32, :],
            send_sem=halo_send.at[n], recv_sem=halo_recv.at[n],
            device_id={"strip": near}, device_id_type=MESH_ID,
        )
        copy.start()
        halos.append(copy)
    build_first(w_first, tile, band_one)
    build_second(w_second, wide, band_two)
    chosen = pick_rows(strip, dy)
    for copy in halos:
        copy.wait_recv()
    slot, group = slot_of(me), group_of(me)

    def start(k):
        @pl.when(me != k)
        def _():
            pltpu.make_async_remote_copy(
                src_ref=send.at[k], dst_ref=recv.at[slot], send_sem=pass_send,
                recv_sem=pass_recv.at[group], device_id={"sec": k}, device_id_type=MESH_ID,
            ).start()

    cut_windows(dot_nn(chosen, ext[...]), send, start)
    pltpu.make_async_copy(send.at[me], recv.at[slot], pass_recv.at[group]).start()
    build_third(w_third, wide, band_three)
    build_fourth(w_fourth, wide, band_four)
    gain_a, gain_b = build_gain(gain_one, tile), build_gain(gain_two, tile)

    def arrived(g):
        pltpu.make_async_copy(
            send.at[0:HALF], recv.at[HALF * g : HALF * g + HALF], pass_recv.at[g]
        ).wait()

    layers(
        arrived, recv, offsets, gain_a, gain_b, strip, me, band_one, band_two, band_three,
        band_four, stage, lhs, big_one, big_two, big_three, square_one, square_two, level, columns,
        middle, out,
    )
    pltpu.make_async_copy(send.at[0 : SECS - 1], recv.at[0 : SECS - 1], pass_send).wait()
    for copy in halos:
        copy.wait_send()


def shards(raw_image, w_first, gain_one, w_second, gain_two, offsets, w_third, w_fourth):
    hbm = pl.BlockSpec(memory_space=pltpu.HBM)
    result = pl.pallas_call(
        kernel,
        out_shape=jax.ShapeDtypeStruct((SECS, ROWS, C * BLOCK), F32),
        in_specs=[hbm] * 8,
        out_specs=pl.BlockSpec(memory_space=pltpu.VMEM),
        scratch_shapes=[
            pltpu.VMEM((9, C), BF16),
            pltpu.VMEM((1, C), F32),
            pltpu.VMEM((3, C, 96), BF16),
            pltpu.VMEM((1, C), F32),
            pltpu.VMEM((2, SECS), jnp.int32),
            pltpu.VMEM((9, C, 96), BF16),
            pltpu.VMEM((9, C, 96), BF16),
            pltpu.SMEM((2, SECS), jnp.int32),
            pltpu.VMEM((32, RAW), BF16),
            pltpu.VMEM((96, RAW + 128), BF16),
            pltpu.VMEM((SECS, 16, 128), BF16),
            pltpu.VMEM((SECS, 16, 128), BF16),
            pltpu.VMEM((2, 256, 512), BF16),
            pltpu.VMEM((2, 256, 768), BF16),
            pltpu.VMEM((9, 256, 256), BF16),
            pltpu.VMEM((3, 256, 1024), BF16),
            pltpu.VMEM((16, 128), F32),
            pltpu.VMEM((C, 256), F32),
            pltpu.VMEM((2, HALF * 16, 128), F32),
            pltpu.VMEM((2, 11 * HALF, 256), BF16),
            pltpu.VMEM((2, 22 * HALF, 512), F32),
            pltpu.VMEM((2, 20 * HALF, 384), F32),
            pltpu.VMEM((576, 384), F32),
            pltpu.VMEM((2, 22 * HALF, 512), BF16),
            pltpu.VMEM((2, 20 * HALF, 384), BF16),
            pltpu.VMEM((2, 22 * HALF, 512), BF16),
            pltpu.VMEM((640, 1152), BF16),
            pltpu.VMEM((576, 1024), BF16),
            pltpu.SemaphoreType.DMA((9,)),
            pltpu.SemaphoreType.DMA((2,)),
            pltpu.SemaphoreType.DMA((2,)),
            pltpu.SemaphoreType.DMA,
            pltpu.SemaphoreType.DMA((2,)),
        ],
        compiler_params=pltpu.CompilerParams(
            collective_id=0, has_side_effects=True, vmem_limit_bytes=48 * 2**20
        ),
        cost_estimate=pl.CostEstimate(flops=10**9, bytes_accessed=2**20, transcendentals=10**6),
    )(
        *[
            pltpu.with_memory_space_constraint(x, pltpu.HBM)
            for x in (
                raw_image.reshape(32, RAW), w_first, gain_one.reshape(1, C), w_second,
                gain_two.reshape(1, C), offsets.T, w_third, w_fourth,
            )
        ]
    )
    return result.reshape(1, SECS, ROWS, C * BLOCK)


def solution(mesh):
    placed = (P("sec", "strip", None), P(), P(), P(), P(), P(), P(), P())
    return jax.shard_map(
        shards, mesh=mesh, in_specs=placed, out_specs=P("sec", None, "strip", None), check_vma=False
    )
```
